32 devices in a mesh: groups: 2 (over x), box: 16 (over z, y, core).
Axes of the slice: x: 2, y: 2, z: 4, core: 2. Of those that a mesh axis runs over, the one named last changes fastest.
Arguments:
- scene_image: bfloat16 [32768, 512], P(('groups', 'box')), parts along dimension 0, may hold values from -6 to 6
- echoes: bfloat16 [32768, 1024], P(('groups', 'box')), parts along dimension 0, may hold values from -6 to 6
- pixel_slot: int32 [32, 1024], P(('groups', 'box')), parts along dimension 0, may hold values from 0 to 1023, each once within a row
- pulse_slot: int32 [32, 1024], P(('groups', 'box')), parts along dimension 0, may hold values from 0 to 1023, each once within a row
- level_perm: int32 [4, 16, 1024], P(None, 'box'), may hold values from 0 to 1023, each once within a row
- target_leaf: bfloat16 [512, 128], replicated, may hold values from -0.25 to 0.25
- source_leaf: bfloat16 [128, 1024], replicated, may hold values from -0.5 to 0.5
- panels: bfloat16 [4, 16, 4, 128, 128], P(None, 'box'), may hold values from -0.375 to 0.375
Outputs:
- new_image: bfloat16 [32768, 512], P(('groups', 'box')), parts along dimension 0
The draws below stay inside these ranges and needn't reach their ends.
There are 2 independent parts, one for each index of `groups`. The reference program is written for one: setup_inputs(seed, part) draws one part's arguments, and reference() takes and returns one part's arrays. A program takes and returns all parts, laid end to end along the dimension named above; an argument that names none is the same for every part. Nothing has to cross between parts.
Inputs may be any that keep to these rules, and one draw needn't show every extreme that they name: `pixel_slot`: each box's row is a permutation of 0 .. 1023. `pulse_slot`: each box's row is a permutation of 0 .. 1023. `level_perm`: each level's row for each box is a permutation of 0 .. 1023.
All inputs are finite; a program needn't handle non-finite values.
Results may differ from the reference program's by a relative error of at most 0.012.
Values may be sent and summed in bfloat16 or wider, within the bound.
No kernel may reach another device: no remote copies, remote signals or barrier semaphores. Data moves between devices by JAX's collectives and lax.ppermute only.
A program may use at most 64 MiB of HBM per device.

```python
import jax
import jax.numpy as jnp
from jax import lax

C = 128
PIXEL_SAMPLES = 512
ECHO_SAMPLES = 1024
ROWS_DEV = 1024
LEVELS = 4
ROWS = 16384
N_BOX = 16


def levels(own_key, dims, cuts, least, top_value):
    def one(axis_at, blocks):
        heights = jax.random.uniform(jax.random.fold_in(jax.random.fold_in(own_key, 6), axis_at), (blocks,), jnp.float32, least / len(cuts), top_value / len(cuts))
        return jnp.repeat(jnp.exp(heights), dims[axis_at] // blocks).reshape((-1,) + (1,) * (len(dims) - axis_at - 1))

    loudness = one(*cuts[0])
    for cut in cuts[1:]:
        loudness = loudness * one(*cut)
    return loudness


def scatter_about(rng, shape, scale, limit, cuts=(), dtype=jnp.bfloat16):
    level = levels(rng, shape, cuts, -0.22, 0.18) if cuts else 1.0
    values = jax.random.normal(rng, shape, jnp.float32) * scale * level
    return jnp.minimum(jnp.maximum(values, -limit), limit).astype(dtype)


def setup_inputs(seed: int = 0, part: int = 0) -> dict:
    seeds = jax.random.split(jax.random.key(seed), 9)
    part_splits = jax.random.split(jax.random.fold_in(seeds[8], part), 9)
    scene_image = scatter_about(part_splits[0], (ROWS, PIXEL_SAMPLES), 1.0, 6.0, ((0, 16),))
    echoes = scatter_about(part_splits[1], (ROWS, ECHO_SAMPLES), 1.0, 6.0, ((0, 16),))
    pixel_slot = jax.vmap(lambda own: jax.random.permutation(own, ROWS_DEV))(jax.random.split(part_splits[2], N_BOX)).reshape((N_BOX, ROWS_DEV)).astype(jnp.int32)
    pulse_slot = jax.vmap(lambda own: jax.random.permutation(own, ROWS_DEV))(jax.random.split(part_splits[3], N_BOX)).reshape((N_BOX, ROWS_DEV)).astype(jnp.int32)
    level_perm = jax.vmap(lambda own: jax.random.permutation(own, ROWS_DEV))(jax.random.split(seeds[4], LEVELS * N_BOX)).reshape((LEVELS, N_BOX, ROWS_DEV)).astype(jnp.int32)
    target_leaf = scatter_about(seeds[5], (PIXEL_SAMPLES, C), PIXEL_SAMPLES ** -0.5, 0.25)
    source_leaf = scatter_about(seeds[6], (C, ECHO_SAMPLES), C ** -0.5, 0.5)
    panels = scatter_about(seeds[7], (LEVELS, N_BOX, 4, C, C), (2 * C) ** -0.5, 0.375, ((1, 16),))
    return {"scene_image": scene_image, "echoes": echoes, "pixel_slot": pixel_slot, "pulse_slot": pulse_slot, "level_perm": level_perm, "target_leaf": target_leaf, "source_leaf": source_leaf, "panels": panels}


step_size = 0.1


def split_pairs(permuted, stride):
    boxes, rows_dev, width = permuted.shape
    half_rows = rows_dev // 2
    groups = boxes // (2 * stride)
    shaped = permuted.reshape(groups, 2, stride, rows_dev, width)
    pieces = []
    for member in range(2):
        part_rows = shaped[:, member].reshape(groups, stride, 2, half_rows, width)
        pieces.append(jnp.swapaxes(part_rows, 1, 2).reshape(boxes, half_rows, width))
    return pieces[0], pieces[1]


def join_pairs(first_grad, second_grad, stride):
    boxes, half_rows, width = first_grad.shape
    groups = boxes // (2 * stride)
    pieces = []
    for member_grad in (first_grad, second_grad):
        shaped = member_grad.reshape(groups, 2, stride, half_rows, width)
        pieces.append(jnp.swapaxes(shaped, 1, 2).reshape(groups, stride, 2 * half_rows, width))
    return jnp.stack(pieces, axis=1).reshape(boxes, 2 * half_rows, width)


def scatter_rows(values, slots):
    return jax.vmap(lambda value_rows, slot_rows: jnp.zeros_like(value_rows).at[slot_rows].set(value_rows))(values, slots)


def reference(scene_image, echoes, pixel_slot, pulse_slot, level_perm, target_leaf, source_leaf, panels):
    boxes = N_BOX
    rows_dev = ROWS_DEV
    half_rows = rows_dev // 2
    leafed = jnp.dot(scene_image, target_leaf, preferred_element_type=jnp.float32).reshape(boxes, rows_dev, -1)
    coefficients = jnp.take_along_axis(leafed, pixel_slot[:, :, None], axis=1).astype(jnp.bfloat16)
    for level_index in range(LEVELS):
        stride = 2 ** level_index
        permuted = jnp.take_along_axis(coefficients, level_perm[level_index][:, :, None], axis=1)
        first, second = split_pairs(permuted, stride)
        first = first.astype(jnp.float32)
        second = second.astype(jnp.float32)
        blocks = panels[level_index].astype(jnp.float32)
        upper = jnp.einsum('bhc,bcd->bhd', first, blocks[:, 0]) + jnp.einsum('bhc,bcd->bhd', second, blocks[:, 1])
        lower = jnp.einsum('bhc,bcd->bhd', first, blocks[:, 2]) + jnp.einsum('bhc,bcd->bhd', second, blocks[:, 3])
        coefficients = jnp.concatenate([upper, lower], axis=1).astype(jnp.bfloat16)
    echo_boxes = echoes.reshape(boxes, rows_dev, -1)

    def pulse_box(entries):
        coef_rows, echo_rows, slot_rows = entries
        predicted = jnp.dot(coef_rows, source_leaf, preferred_element_type=jnp.float32)
        residual = (predicted[slot_rows] - echo_rows.astype(jnp.float32)).astype(jnp.bfloat16)
        backward = lax.dot_general(residual, source_leaf, (((1,), (1,)), ((), ())), preferred_element_type=jnp.float32)
        return jnp.zeros_like(backward).at[slot_rows].set(backward).astype(jnp.bfloat16)

    coefficients = lax.map(pulse_box, (coefficients, echo_boxes, pulse_slot))
    for level_index in reversed(range(LEVELS)):
        stride = 2 ** level_index
        blocks = panels[level_index].astype(jnp.float32)
        top_rows = coefficients[:, :half_rows].astype(jnp.float32)
        bottom_rows = coefficients[:, half_rows:].astype(jnp.float32)
        first_grad = (jnp.einsum('bhd,bcd->bhc', top_rows, blocks[:, 0]) + jnp.einsum('bhd,bcd->bhc', bottom_rows, blocks[:, 2])).astype(jnp.bfloat16)
        second_grad = (jnp.einsum('bhd,bcd->bhc', top_rows, blocks[:, 1]) + jnp.einsum('bhd,bcd->bhc', bottom_rows, blocks[:, 3])).astype(jnp.bfloat16)
        permuted_grad = join_pairs(first_grad, second_grad, stride)
        coefficients = scatter_rows(permuted_grad, level_perm[level_index])
    pixel_coefs = scatter_rows(coefficients, pixel_slot).reshape(boxes * rows_dev, -1)
    gradient = lax.dot_general(pixel_coefs, target_leaf, (((1,), (1,)), ((), ())), preferred_element_type=jnp.float32)
    return (scene_image.astype(jnp.float32) - step_size * gradient).astype(jnp.bfloat16)
```

```python
import functools

import jax
import jax.numpy as jnp
from jax import lax
from jax.experimental import pallas as pl
from jax.experimental.pallas import tpu as pltpu
from jax.sharding import PartitionSpec as P

step_size = 0.1
wide = jnp.float32
thin = jnp.bfloat16
lanes = 128
depth = 256


def swapped(value, axis, apart):
    return lax.ppermute(value, axis, [(i, i ^ 1 << apart) for i in range(lax.axis_size(axis))])


def mul(left, right):
    return jnp.dot(left, right, preferred_element_type=wide)


def mul_t(left, right):
    return lax.dot_general(left, right, (((1,), (1,)), ((), ())), preferred_element_type=wide)


def bit_of(level):
    return lax.axis_index("box") // 2**level % 2


def half_row(row_ref, bit):
    half = row_ref.shape[1] // 2
    return row_ref[:, pl.ds(pl.multiple_of(bit * half, half), half)]


def column(row):
    parts = []
    for at in range(0, row.shape[1], lanes):
        parts.append(jnp.broadcast_to(row[:, at : at + lanes], (lanes, lanes)).T)
    return jnp.concatenate(parts, axis=0)


def one_hot(hits):
    return jnp.where(hits, 1.0, 0.0).astype(thin)


def take(row, values):
    slots = column(row)
    lane = lax.broadcasted_iota(jnp.int32, slots.shape, 1)
    total = None
    for at in range(0, values.shape[0], depth):
        chosen = jnp.concatenate(
            [one_hot(slots == lane + (at + more)) for more in range(0, depth, lanes)], axis=1
        )
        part = mul(chosen, values[at : at + depth])
        total = part if total is None else total + part
    return total


def place(row, values, rows):
    total = None
    target = lax.broadcasted_iota(jnp.int32, (rows, depth), 0)
    for at in range(0, values.shape[0], depth):
        chosen = one_hot(target == row[:, at : at + depth])
        part = mul(chosen, values[at : at + depth])
        total = part if total is None else total + part
    return total


def compose(outer, inner):
    digits = jnp.concatenate([outer // 256, outer % 256], axis=0).astype(wide)
    digits = jnp.pad(digits, ((0, 14), (0, 0))).astype(thin)
    total = None
    target = lax.broadcasted_iota(jnp.int32, (depth, inner.shape[1]), 0)
    for at in range(0, outer.shape[1], depth):
        chosen = one_hot(target + at == inner)
        part = mul(digits[:, at : at + depth], chosen)
        total = part if total is None else total + part
    return (total[0:1] * 256 + total[1:2]).astype(jnp.int32)


def stack(values):
    half = values.shape[0] // 2
    return jnp.concatenate([values[:half], values[half:]], axis=1)


def unstack(values):
    width = values.shape[1] // 2
    return jnp.concatenate([values[:, :width], values[:, width:]], axis=0)


def pair_weight(panel_ref, which):
    return jnp.concatenate([panel_ref[0, which], panel_ref[0, 2 + which]], axis=1)


def first_kernel(scene_ref, leaf_ref, pixel_ref, perm_ref, leafed_ref, slots_ref, out_ref):
    slots = compose(pixel_ref[...], half_row(perm_ref, 1 - bit_of(0)))
    slots_ref[...] = slots
    leafed = mul(scene_ref[...], leaf_ref[...]).astype(thin)
    leafed_ref[...] = leafed
    out_ref[...] = take(slots, leafed).astype(thin)


def first_own_kernel(leafed_ref, pixel_ref, perm_ref, panel_ref, slots_ref, part_ref):
    bit = bit_of(0)
    slots = compose(pixel_ref[...], half_row(perm_ref, bit))
    slots_ref[...] = slots
    own = take(slots, leafed_ref[...]).astype(thin)
    part_ref[...] = mul(own, pair_weight(panel_ref, bit))


def own_kernel(level, coef_ref, perm_ref, panel_ref, part_ref):
    bit = bit_of(level)
    own = take(half_row(perm_ref, bit), coef_ref[...]).astype(thin)
    part_ref[...] = mul(own, pair_weight(panel_ref, bit))


def mix(level, arrived_ref, part_ref, panel_ref):
    mixture = part_ref[...] + mul(arrived_ref[...], pair_weight(panel_ref, 1 - bit_of(level)))
    return unstack(mixture.astype(thin))


def forward_kernel(level, arrived_ref, part_ref, panel_ref, perm_ref, coef_ref, out_ref):
    coefficients = mix(level, arrived_ref, part_ref, panel_ref)
    coef_ref[...] = coefficients
    out_ref[...] = take(half_row(perm_ref, 1 - bit_of(level + 1)), coefficients).astype(thin)


def echo_kernel(echo_ref, leaf_ref, slots_ref, back_ref, gram_ref):
    leaf = leaf_ref[...]
    gram = mul_t(leaf, leaf)
    high = gram.astype(thin)
    low = (gram - high.astype(wide)).astype(thin)
    gram_ref[...] = jnp.concatenate([high, low], axis=0)
    back = mul_t(echo_ref[...], leaf).astype(thin)
    back_ref[...] = place(slots_ref[...], back, back.shape[0])


def centre_kernel(level, arrived_ref, part_ref, panel_ref, echo_ref, gram_ref, coef_ref, out_ref):
    coefficients = mix(level, arrived_ref, part_ref, panel_ref)
    twice = jnp.concatenate([coefficients, coefficients], axis=1)
    back = (mul(twice, gram_ref[...]) - echo_ref[...]).astype(thin)
    coef_ref[...] = back
    out_ref[...] = mul_t(stack(back), pair_weight(panel_ref, 1 - bit_of(level))).astype(thin)


def own_back_kernel(level, coef_ref, panel_ref, perm_ref, placed_ref):
    bit = bit_of(level)
    own = mul_t(stack(coef_ref[...]), pair_weight(panel_ref, bit)).astype(thin)
    row = perm_ref[...] if perm_ref.shape[1] == own.shape[0] else half_row(perm_ref, bit)
    placed_ref[...] = place(row, own, coef_ref.shape[0]).astype(thin)


def backward_kernel(level, arrived_ref, placed_ref, perm_ref, panel_ref, coef_ref, out_ref):
    row = half_row(perm_ref, 1 - bit_of(level + 1))
    back = place(row, arrived_ref[...], placed_ref.shape[0]) + placed_ref[...].astype(wide)
    back = back.astype(thin)
    coef_ref[...] = back
    out_ref[...] = mul_t(stack(back), pair_weight(panel_ref, 1 - bit_of(level))).astype(thin)


def last_kernel(arrived_ref, placed_ref, slots_ref, leaf_ref, scene_ref, image_ref):
    back = place(slots_ref[...], arrived_ref[...], placed_ref.shape[0])
    back = (back + placed_ref[...].astype(wide)).astype(thin)
    gradient = mul_t(back, leaf_ref[...])
    image_ref[...] = (scene_ref[...].astype(wide) - step_size * gradient).astype(thin)


def call(kernel, outs, *operands, work=1):
    whole = pl.BlockSpec(memory_space=pltpu.VMEM)
    shapes = tuple(jax.ShapeDtypeStruct(shape, kind) for shape, kind in outs)
    got = pl.pallas_call(
        kernel,
        out_shape=shapes,
        in_specs=[whole] * len(operands),
        out_specs=tuple(whole for _ in shapes),
        compiler_params=pltpu.CompilerParams(vmem_limit_bytes=16 * 2**20),
        cost_estimate=pl.CostEstimate(
            flops=work * 10**8, bytes_accessed=10**6, transcendentals=0
        ),
    )(*operands)
    return got[0] if len(outs) == 1 else got


def on_device(
    scene_image, echoes, pixel_slot, pulse_slot, level_perm, target_leaf, source_leaf, panels
):
    levels = lax.axis_size("box").bit_length() - 1
    rows = scene_image.shape[0]
    half = rows // 2
    width = target_leaf.shape[1]
    column_of = ((rows, width), thin)
    row_half = ((1, half), jnp.int32)
    sent = ((half, width), thin)
    mixed = ((half, 2 * width), wide)
    perms = [level_perm[level] for level in range(levels)]
    blocks = [panels[level] for level in range(levels)]

    leafed, out_slots, outgoing = call(
        first_kernel, [column_of, row_half, sent], scene_image, target_leaf, pixel_slot, perms[0]
    )
    arrived = swapped(outgoing, "box", 0)
    own_slots, part = call(
        first_own_kernel, [row_half, mixed], leafed, pixel_slot, perms[0], blocks[0]
    )
    for level in range(1, levels):
        coefficients, outgoing = call(
            functools.partial(forward_kernel, level - 1),
            [column_of, sent],
            arrived,
            part,
            blocks[level - 1],
            perms[level],
        )
        arrived = swapped(outgoing, "box", level)
        part = call(
            functools.partial(own_kernel, level),
            [mixed],
            coefficients,
            perms[level],
            blocks[level],
        )

    echo_back, gram = call(
        echo_kernel,
        [((rows, width), wide), ((2 * width, width), thin)],
        echoes,
        source_leaf,
        pulse_slot,
    )
    last = levels - 1
    coefficients, outgoing = call(
        functools.partial(centre_kernel, last),
        [column_of, sent],
        arrived,
        part,
        blocks[last],
        echo_back,
        gram,
    )
    for level in reversed(range(levels)):
        arrived = swapped(outgoing, "box", level)
        placed = call(
            functools.partial(own_back_kernel, level),
            [column_of],
            coefficients,
            blocks[level],
            perms[level] if level else own_slots,
        )
        if level:
            coefficients, outgoing = call(
                functools.partial(backward_kernel, level - 1),
                [column_of, sent],
                arrived,
                placed,
                perms[level],
                blocks[level - 1],
            )
    return call(
        last_kernel,
        [((rows, scene_image.shape[1]), thin)],
        arrived,
        placed,
        out_slots,
        target_leaf,
        scene_image,
    )


def solution(mesh):
    return jax.shard_map(
        on_device,
        mesh=mesh,
        in_specs=(
            P(("groups", "box"), None),
            P(("groups", "box"), None),
            P(("groups", "box"), None),
            P(("groups", "box"), None),
            P(None, "box", None),
            P(),
            P(),
            P(None, "box", None, None, None),
        ),
        out_specs=P(("groups", "box"), None),
        check_vma=False,
    )
```

```python
import functools

import jax
import jax.numpy as jnp
from jax import lax
from jax.experimental import pallas as pl
from jax.experimental.pallas import tpu as pltpu
from jax.sharding import PartitionSpec as P

step_size = 0.1
wide = jnp.float32
thin = jnp.bfloat16
lanes = 128
depth = 256
scene_chunks = 4


def swapped(value, axis, apart):
    return lax.ppermute(value, axis, [(i, i ^ 1 << apart) for i in range(lax.axis_size(axis))])


def mul(left, right):
    return jnp.dot(left, right, preferred_element_type=wide)


def mul_t(left, right):
    return lax.dot_general(left, right, (((1,), (1,)), ((), ())), preferred_element_type=wide)


def bit_of(level):
    return lax.axis_index("box") // 2**level % 2


def half_row(perm_ref, level, which):
    half = perm_ref.shape[2] // 2
    return perm_ref[level, :, pl.ds(pl.multiple_of(which * half, half), half)]


def column(row):
    parts = []
    for at in range(0, row.shape[1], lanes):
        parts.append(jnp.broadcast_to(row[:, at : at + lanes], (lanes, lanes)).T)
    return jnp.concatenate(parts, axis=0)


def one_hot(hits):
    return jnp.where(hits, 1.0, 0.0).astype(thin)


def take(row, values):
    slots = column(row)
    lane = lax.broadcasted_iota(jnp.int32, slots.shape, 1)
    total = None
    for at in range(0, values.shape[0], depth):
        chosen = jnp.concatenate(
            [one_hot(slots == lane + (at + more)) for more in range(0, depth, lanes)], axis=1
        )
        part = mul(chosen, values[at : at + depth])
        total = part if total is None else total + part
    return total


def place(row, values, rows):
    total = None
    target = lax.broadcasted_iota(jnp.int32, (rows, depth), 0)
    for at in range(0, values.shape[0], depth):
        chosen = one_hot(target == row[:, at : at + depth])
        part = mul(chosen, values[at : at + depth])
        total = part if total is None else total + part
    return total


def compose(outer, inner):
    digits = jnp.concatenate([outer // 256, outer % 256], axis=0).astype(wide)
    digits = jnp.pad(digits, ((0, 14), (0, 0))).astype(thin)
    total = None
    target = lax.broadcasted_iota(jnp.int32, (depth, inner.shape[1]), 0)
    for at in range(0, outer.shape[1], depth):
        chosen = one_hot(target + at == inner)
        part = mul(digits[:, at : at + depth], chosen)
        total = part if total is None else total + part
    return (total[0:1] * 256 + total[1:2]).astype(jnp.int32)


def stack(values):
    half = values.shape[0] // 2
    return jnp.concatenate([values[:half], values[half:]], axis=1)


def unstack(values):
    width = values.shape[1] // 2
    return jnp.concatenate([values[:, :width], values[:, width:]], axis=0)


def pair_weight(panel_ref, level, which):
    return jnp.concatenate(
        [panel_ref[level, 0, which], panel_ref[level, 0, 2 + which]], axis=1
    )


def first_kernel(
    scene_in, leaf_in, pixel_in, perm_in, panel_in,
    scene_ref, leaf_ref, pixel_ref, perm_ref, panel_ref, leafed_ref, slots_ref, out_ref, done,
):
    rows = scene_ref.shape[0]
    half = rows // 2
    chunk = rows // scene_chunks
    parts = [pl.ds(at * chunk, chunk) for at in range(scene_chunks)]
    pairs = [(pixel_in, pixel_ref), (perm_in, perm_ref), (leaf_in, leaf_ref)]
    pairs += [(scene_in.at[part], scene_ref.at[part]) for part in parts]
    pairs += [(panel_in, panel_ref)]
    loads = [
        pltpu.make_async_copy(source, target, done.at[at])
        for at, (source, target) in enumerate(pairs)
    ]
    for load in loads:
        load.start()
    loads[0].wait()
    loads[1].wait()
    slots = compose(pixel_ref[...], half_row(perm_ref, 0, 1 - bit_of(0)))
    slots_ref[...] = slots
    loads[2].wait()
    for at, part in enumerate(parts):
        loads[3 + at].wait()
        leafed_ref[part] = mul(scene_ref[part], leaf_ref[...]).astype(thin)
    out_ref[...] = take(slots, leafed_ref[...]).astype(thin)
    loads[-1].wait()


def first_own_kernel(leafed_ref, pixel_ref, perm_ref, panel_ref, slots_ref, part_ref):
    bit = bit_of(0)
    slots = compose(pixel_ref[...], half_row(perm_ref, 0, bit))
    slots_ref[...] = slots
    own = take(slots, leafed_ref[...]).astype(thin)
    part_ref[...] = mul(own, pair_weight(panel_ref, 0, bit))


def own_kernel(level, coef_ref, perm_ref, panel_ref, part_ref):
    bit = bit_of(level)
    own = take(half_row(perm_ref, level, bit), coef_ref[...]).astype(thin)
    part_ref[...] = mul(own, pair_weight(panel_ref, level, bit))


def own_echo_kernel(
    level, coef_ref, perm_ref, panel_ref, echo_in, leaf_in, slots_in,
    part_ref, back_ref, gram_ref, echo, leaf, slots, done,
):
    rows = coef_ref.shape[0]
    chunk = rows // scene_chunks
    parts = [pl.ds(at * chunk, chunk) for at in range(scene_chunks)]
    pairs = [(slots_in, slots), (leaf_in, leaf)]
    pairs += [(echo_in.at[part], echo.at[part]) for part in parts]
    loads = [
        pltpu.make_async_copy(source, target, done.at[at])
        for at, (source, target) in enumerate(pairs)
    ]
    for load in loads:
        load.start()
    own_kernel(level, coef_ref, perm_ref, panel_ref, part_ref)
    loads[0].wait()
    loads[1].wait()
    gram = mul_t(leaf[...], leaf[...])
    high = gram.astype(thin)
    low = (gram - high.astype(wide)).astype(thin)
    gram_ref[...] = jnp.concatenate([high, low], axis=0)
    back = []
    for at, part in enumerate(parts):
        loads[2 + at].wait()
        back.append(mul_t(echo[part], leaf[...]).astype(thin))
    back_ref[...] = place(slots[...], jnp.concatenate(back, axis=0), rows)


def mix(level, arrived_ref, part_ref, panel_ref):
    weight = pair_weight(panel_ref, level, 1 - bit_of(level))
    mixture = part_ref[...] + mul(arrived_ref[...], weight)
    return unstack(mixture.astype(thin))


def forward_kernel(level, arrived_ref, part_ref, panel_ref, perm_ref, coef_ref, out_ref):
    coefficients = mix(level, arrived_ref, part_ref, panel_ref)
    coef_ref[...] = coefficients
    slots = half_row(perm_ref, level + 1, 1 - bit_of(level + 1))
    out_ref[...] = take(slots, coefficients).astype(thin)


def centre_kernel(level, arrived_ref, part_ref, panel_ref, echo_ref, gram_ref, coef_ref, out_ref):
    coefficients = mix(level, arrived_ref, part_ref, panel_ref)
    twice = jnp.concatenate([coefficients, coefficients], axis=1)
    back = (mul(twice, gram_ref[...]) - echo_ref[...]).astype(thin)
    coef_ref[...] = back
    weight = pair_weight(panel_ref, level, 1 - bit_of(level))
    out_ref[...] = mul_t(stack(back), weight).astype(thin)


def own_back_kernel(level, coef_ref, panel_ref, perm_ref, placed_ref):
    bit = bit_of(level)
    own = mul_t(stack(coef_ref[...]), pair_weight(panel_ref, level, bit)).astype(thin)
    row = half_row(perm_ref, level, bit) if level else perm_ref[...]
    placed_ref[...] = place(row, own, coef_ref.shape[0]).astype(thin)


def backward_kernel(level, arrived_ref, placed_ref, perm_ref, panel_ref, coef_ref, out_ref):
    row = half_row(perm_ref, level + 1, 1 - bit_of(level + 1))
    back = place(row, arrived_ref[...], placed_ref.shape[0]) + placed_ref[...].astype(wide)
    back = back.astype(thin)
    coef_ref[...] = back
    weight = pair_weight(panel_ref, level, 1 - bit_of(level))
    out_ref[...] = mul_t(stack(back), weight).astype(thin)


def last_kernel(arrived_ref, placed_ref, slots_ref, leaf_ref, scene_ref, image_ref, image, sent):
    rows = scene_ref.shape[0]
    chunk = rows // scene_chunks
    back = place(slots_ref[...], arrived_ref[...], rows)
    back = (back + placed_ref[...].astype(wide)).astype(thin)
    stores = []
    for at in range(scene_chunks):
        part = pl.ds(at * chunk, chunk)
        gradient = mul_t(back[at * chunk : (at + 1) * chunk], leaf_ref[...])
        image[part] = (scene_ref[part].astype(wide) - step_size * gradient).astype(thin)
        stores.append(pltpu.make_async_copy(image.at[part], image_ref.at[part], sent.at[at]))
        stores[-1].start()
    for store in stores:
        store.wait()


def call(kernel, outs, *operands, far=(), far_out=False, scratch=()):
    shapes = tuple(jax.ShapeDtypeStruct(shape, kind) for shape, kind in outs)
    near, off = pl.BlockSpec(memory_space=pltpu.VMEM), pl.BlockSpec(memory_space=pltpu.HBM)
    away = tuple(pltpu.with_memory_space_constraint(array, pltpu.HBM) for array in far)
    got = pl.pallas_call(
        kernel,
        out_shape=shapes,
        in_specs=[near] * len(operands) + [off] * len(far),
        out_specs=tuple(off if far_out else near for _ in shapes),
        scratch_shapes=scratch,
        compiler_params=pltpu.CompilerParams(vmem_limit_bytes=16 * 2**20),
        cost_estimate=pl.CostEstimate(flops=10**8, bytes_accessed=10**6, transcendentals=0),
    )(*operands, *away)
    return got[0] if len(outs) == 1 else got


def like(array):
    return (array.shape, array.dtype)


def on_device(
    scene_image, echoes, pixel_slot, pulse_slot, level_perm, target_leaf, source_leaf, panels
):
    levels = lax.axis_size("box").bit_length() - 1
    rows, samples = scene_image.shape
    half = rows // 2
    width = target_leaf.shape[1]
    column_of = ((rows, width), thin)
    row_half = ((1, half), jnp.int32)
    sent = ((half, width), thin)
    mixed = ((half, 2 * width), wide)

    far = (scene_image, target_leaf, pixel_slot, level_perm, panels)
    scene_near, leaf_near, pixel_near, perms, blocks, leafed, out_slots, outgoing = call(
        first_kernel,
        [like(array) for array in far] + [column_of, row_half, sent],
        far=far,
        scratch=[pltpu.SemaphoreType.DMA((4 + scene_chunks,))],
    )
    arrived = swapped(outgoing, "box", 0)
    own_slots, part = call(
        first_own_kernel, [row_half, mixed], leafed, pixel_near, perms, blocks
    )
    for level in range(1, levels):
        coefficients, outgoing = call(
            functools.partial(forward_kernel, level - 1),
            [column_of, sent],
            arrived,
            part,
            blocks,
            perms,
        )
        arrived = swapped(outgoing, "box", level)
        if level == 1:
            part, echo_back, gram = call(
                functools.partial(own_echo_kernel, level),
                [mixed, ((rows, width), wide), ((2 * width, width), thin)],
                coefficients,
                perms,
                blocks,
                far=(echoes, source_leaf, pulse_slot),
                scratch=[
                    pltpu.VMEM(echoes.shape, thin),
                    pltpu.VMEM(source_leaf.shape, thin),
                    pltpu.VMEM(pulse_slot.shape, jnp.int32),
                    pltpu.SemaphoreType.DMA((2 + scene_chunks,)),
                ],
            )
        else:
            part = call(
                functools.partial(own_kernel, level), [mixed], coefficients, perms, blocks
            )

    last = levels - 1
    coefficients, outgoing = call(
        functools.partial(centre_kernel, last),
        [column_of, sent],
        arrived,
        part,
        blocks,
        echo_back,
        gram,
    )
    for level in reversed(range(levels)):
        arrived = swapped(outgoing, "box", level)
        placed = call(
            functools.partial(own_back_kernel, level),
            [column_of],
            coefficients,
            blocks,
            perms if level else own_slots,
        )
        if level:
            coefficients, outgoing = call(
                functools.partial(backward_kernel, level - 1),
                [column_of, sent],
                arrived,
                placed,
                perms,
                blocks,
            )
    return call(
        last_kernel,
        [((rows, samples), thin)],
        arrived,
        placed,
        out_slots,
        leaf_near,
        scene_near,
        far_out=True,
        scratch=[
            pltpu.VMEM((rows, samples), thin),
            pltpu.SemaphoreType.DMA((scene_chunks,)),
        ],
    )


def solution(mesh):
    return jax.shard_map(
        on_device,
        mesh=mesh,
        in_specs=(
            P(("groups", "box"), None),
            P(("groups", "box"), None),
            P(("groups", "box"), None),
            P(("groups", "box"), None),
            P(None, "box", None),
            P(),
            P(),
            P(None, "box", None, None, None),
        ),
        out_specs=P(("groups", "box"), None),
        check_vma=False,
    )
```

```python
import functools

import jax
import jax.numpy as jnp
from jax import lax
from jax.experimental import pallas as pl
from jax.experimental.pallas import tpu as pltpu
from jax.sharding import PartitionSpec as P

step_size = 0.1
wide = jnp.float32
thin = jnp.bfloat16
lanes = 128
depth = 256
scene_chunks = 4


def swapped(value, axis, apart):
    return lax.ppermute(value, axis, [(i, i ^ 1 << apart) for i in range(lax.axis_size(axis))])


def mul(left, right):
    return jnp.dot(left, right, preferred_element_type=wide)


def mul_t(left, right):
    return lax.dot_general(left, right, (((1,), (1,)), ((), ())), preferred_element_type=wide)


def bit_of(level):
    return lax.axis_index("box") // 2**level % 2


def half_row(perm_ref, level, which):
    half = perm_ref.shape[2] // 2
    return perm_ref[level, :, pl.ds(pl.multiple_of(which * half, half), half)]


def column(row):
    parts = []
    for at in range(0, row.shape[1], lanes):
        parts.append(jnp.broadcast_to(row[:, at : at + lanes], (lanes, lanes)).T)
    return jnp.concatenate(parts, axis=0)


def one_hot(hits):
    return jnp.where(hits, 1.0, 0.0).astype(thin)


def take(row, values):
    slots = column(row)
    lane = lax.broadcasted_iota(jnp.int32, slots.shape, 1)
    total = None
    for at in range(0, values.shape[0], depth):
        chosen = jnp.concatenate(
            [one_hot(slots == lane + (at + more)) for more in range(0, depth, lanes)], axis=1
        )
        part = mul(chosen, values[at : at + depth])
        total = part if total is None else total + part
    return total


def place(row, values, rows):
    total = None
    target = lax.broadcasted_iota(jnp.int32, (rows, depth), 0)
    for at in range(0, values.shape[0], depth):
        chosen = one_hot(target == row[:, at : at + depth])
        part = mul(chosen, values[at : at + depth])
        total = part if total is None else total + part
    return total


def compose(outer, inner):
    digits = jnp.concatenate([outer // 256, outer % 256], axis=0).astype(wide)
    digits = jnp.pad(digits, ((0, 14), (0, 0))).astype(thin)
    total = None
    target = lax.broadcasted_iota(jnp.int32, (depth, inner.shape[1]), 0)
    for at in range(0, outer.shape[1], depth):
        chosen = one_hot(target + at == inner)
        part = mul(digits[:, at : at + depth], chosen)
        total = part if total is None else total + part
    return (total[0:1] * 256 + total[1:2]).astype(jnp.int32)


def stack(values):
    half = values.shape[0] // 2
    return jnp.concatenate([values[:half], values[half:]], axis=1)


def unstack(values):
    width = values.shape[1] // 2
    return jnp.concatenate([values[:, :width], values[:, width:]], axis=0)


def pair_weight(panel_ref, level, which):
    return jnp.concatenate(
        [panel_ref[level, 0, which], panel_ref[level, 0, 2 + which]], axis=1
    )


def pair_weights(panel_ref, level):
    bit = bit_of(level)
    own, other = pair_weight(panel_ref, level, bit), pair_weight(panel_ref, level, 1 - bit)
    return jnp.concatenate([own, other], axis=0)


def first_kernel(
    scene_in, leaf_in, pixel_in, perm_in, panel_in,
    scene_ref, leaf_ref, pixel_ref, perm_ref, panel_ref, leafed_ref, slots_ref, out_ref, done,
):
    rows = scene_ref.shape[0]
    half = rows // 2
    chunk = rows // scene_chunks
    parts = [pl.ds(at * chunk, chunk) for at in range(scene_chunks)]
    pairs = [(pixel_in, pixel_ref), (perm_in, perm_ref), (leaf_in, leaf_ref)]
    pairs += [(scene_in.at[part], scene_ref.at[part]) for part in parts]
    pairs += [(panel_in, panel_ref)]
    loads = [
        pltpu.make_async_copy(source, target, done.at[at])
        for at, (source, target) in enumerate(pairs)
    ]
    for load in loads:
        load.start()
    loads[0].wait()
    loads[1].wait()
    slots = compose(pixel_ref[...], half_row(perm_ref, 0, 1 - bit_of(0)))
    slots_ref[...] = slots
    loads[2].wait()
    for at, part in enumerate(parts):
        loads[3 + at].wait()
        leafed_ref[part] = mul(scene_ref[part], leaf_ref[...]).astype(thin)
    out_ref[...] = take(slots, leafed_ref[...]).astype(thin)
    loads[-1].wait()


def first_own_kernel(leafed_ref, pixel_ref, perm_ref, panel_ref, slots_ref, part_ref):
    bit = bit_of(0)
    slots = compose(pixel_ref[...], half_row(perm_ref, 0, bit))
    slots_ref[...] = slots
    own = take(slots, leafed_ref[...]).astype(thin)
    part_ref[...] = mul(own, pair_weight(panel_ref, 0, bit))


def own_kernel(level, coef_ref, perm_ref, panel_ref, part_ref):
    bit = bit_of(level)
    own = take(half_row(perm_ref, level, bit), coef_ref[...]).astype(thin)
    part_ref[...] = mul(own, pair_weight(panel_ref, level, bit))


def split(values):
    high = values.astype(thin)
    return jnp.concatenate([high, (values - high.astype(wide)).astype(thin)], axis=0)


def twice(values):
    return jnp.concatenate([values, values], axis=1)


def own_map_kernel(
    level, last, coef_ref, perm_ref, panel_ref, echo_in, leaf_in, slots_in,
    part_ref, own_map_ref, other_map_ref, sent_map_ref, back_ref, echo, leaf, slots, done,
):
    rows = coef_ref.shape[0]
    chunk = rows // scene_chunks
    parts = [pl.ds(at * chunk, chunk) for at in range(scene_chunks)]
    pairs = [(slots_in, slots), (leaf_in, leaf)]
    pairs += [(echo_in.at[part], echo.at[part]) for part in parts]
    loads = [
        pltpu.make_async_copy(source, target, done.at[at])
        for at, (source, target) in enumerate(pairs)
    ]
    for load in loads:
        load.start()
    own_kernel(level, coef_ref, perm_ref, panel_ref, part_ref)
    loads[0].wait()
    loads[1].wait()
    gram = split(mul_t(leaf[...], leaf[...]))
    both = pair_weights(panel_ref, last)
    width = both.shape[0] // 2
    scaled = stack(mul(twice(unstack(both)), gram))
    pair = mul_t(split(scaled), both)
    maps = pair[: 2 * width] + pair[2 * width :]
    own_map_ref[...] = split(maps[:width])
    other_map_ref[...] = split(maps[width:, :width])
    sent_map_ref[...] = split(maps[width:, width:])
    back = []
    for at, part in enumerate(parts):
        loads[2 + at].wait()
        back.append(mul_t(echo[part], leaf[...]).astype(thin))
    back_ref[...] = place(slots[...], jnp.concatenate(back, axis=0), rows).astype(thin)


def own_echo_kernel(
    level, last, coef_ref, perm_ref, panel_ref, back_ref, part_ref, echo_part_ref
):
    own_kernel(level, coef_ref, perm_ref, panel_ref, part_ref)
    echo_part_ref[...] = mul_t(stack(back_ref[...]), pair_weights(panel_ref, last))


def mix(level, arrived_ref, part_ref, panel_ref):
    weight = pair_weight(panel_ref, level, 1 - bit_of(level))
    mixture = part_ref[...] + mul(arrived_ref[...], weight)
    return unstack(mixture.astype(thin))


def forward_kernel(level, arrived_ref, part_ref, panel_ref, perm_ref, coef_ref, out_ref):
    coefficients = mix(level, arrived_ref, part_ref, panel_ref)
    coef_ref[...] = coefficients
    slots = half_row(perm_ref, level + 1, 1 - bit_of(level + 1))
    out_ref[...] = take(slots, coefficients).astype(thin)


def bracket_kernel(
    level, coef_ref, perm_ref, map_ref, echo_part_ref, sent_ref, arrived_map_ref,
    part_ref, rest_ref, out_ref,
):
    own = take(half_row(perm_ref, level, bit_of(level)), coef_ref[...]).astype(thin)
    both = mul(twice(own), map_ref[...]) - echo_part_ref[...]
    width = own.shape[1]
    part_ref[...] = both[:, :width]
    out_ref[...] = both[:, width:].astype(thin)
    rest_ref[...] = mul(twice(sent_ref[...]), arrived_map_ref[...])


def join_kernel(level, arrived_ref, part_ref, map_ref, perm_ref, placed_ref):
    own = part_ref[...] + mul(twice(arrived_ref[...]), map_ref[...])
    row = half_row(perm_ref, level, bit_of(level))
    placed_ref[...] = place(row, own.astype(thin), placed_ref.shape[0]).astype(thin)


def own_back_kernel(level, coef_ref, panel_ref, perm_ref, placed_ref):
    bit = bit_of(level)
    own = mul_t(stack(coef_ref[...]), pair_weight(panel_ref, level, bit)).astype(thin)
    row = half_row(perm_ref, level, bit) if level else perm_ref[...]
    placed_ref[...] = place(row, own, coef_ref.shape[0]).astype(thin)


def backward_kernel(level, arrived_ref, placed_ref, perm_ref, panel_ref, *refs):
    *rest_ref, coef_ref, out_ref = refs
    arrived = arrived_ref[...]
    if rest_ref:
        arrived = (arrived.astype(wide) + rest_ref[0][...]).astype(thin)
    row = half_row(perm_ref, level + 1, 1 - bit_of(level + 1))
    back = place(row, arrived, placed_ref.shape[0]) + placed_ref[...].astype(wide)
    back = back.astype(thin)
    coef_ref[...] = back
    weight = pair_weight(panel_ref, level, 1 - bit_of(level))
    out_ref[...] = mul_t(stack(back), weight).astype(thin)


def last_kernel(arrived_ref, placed_ref, slots_ref, leaf_ref, scene_ref, image_ref, image, sent):
    rows = scene_ref.shape[0]
    chunk = rows // scene_chunks
    back = place(slots_ref[...], arrived_ref[...], rows)
    back = (back + placed_ref[...].astype(wide)).astype(thin)
    stores = []
    for at in range(scene_chunks):
        part = pl.ds(at * chunk, chunk)
        gradient = mul_t(back[at * chunk : (at + 1) * chunk], leaf_ref[...])
        image[part] = (scene_ref[part].astype(wide) - step_size * gradient).astype(thin)
        stores.append(pltpu.make_async_copy(image.at[part], image_ref.at[part], sent.at[at]))
        stores[-1].start()
    for store in stores:
        store.wait()


def call(kernel, outs, *operands, far=(), far_out=False, scratch=()):
    shapes = tuple(jax.ShapeDtypeStruct(shape, kind) for shape, kind in outs)
    near, off = pl.BlockSpec(memory_space=pltpu.VMEM), pl.BlockSpec(memory_space=pltpu.HBM)
    away = tuple(pltpu.with_memory_space_constraint(array, pltpu.HBM) for array in far)
    got = pl.pallas_call(
        kernel,
        out_shape=shapes,
        in_specs=[near] * len(operands) + [off] * len(far),
        out_specs=tuple(off if far_out else near for _ in shapes),
        scratch_shapes=scratch,
        compiler_params=pltpu.CompilerParams(vmem_limit_bytes=16 * 2**20),
        cost_estimate=pl.CostEstimate(flops=10**6, bytes_accessed=10**4, transcendentals=0),
    )(*operands, *away)
    return got[0] if len(outs) == 1 else got


def like(array):
    return (array.shape, array.dtype)


def on_device(
    scene_image, echoes, pixel_slot, pulse_slot, level_perm, target_leaf, source_leaf, panels
):
    levels = lax.axis_size("box").bit_length() - 1
    rows, samples = scene_image.shape
    half = rows // 2
    width = target_leaf.shape[1]
    column_of = ((rows, width), thin)
    row_half = ((1, half), jnp.int32)
    sent = ((half, width), thin)
    mixed = ((half, 2 * width), wide)

    far = (scene_image, target_leaf, pixel_slot, level_perm, panels)
    scene_near, leaf_near, pixel_near, perms, blocks, leafed, out_slots, outgoing = call(
        first_kernel,
        [like(array) for array in far] + [column_of, row_half, sent],
        far=far,
        scratch=[pltpu.SemaphoreType.DMA((4 + scene_chunks,))],
    )
    arrived = swapped(outgoing, "box", 0)
    own_slots, part = call(
        first_own_kernel, [row_half, mixed], leafed, pixel_near, perms, blocks
    )
    last = levels - 1
    for level in range(1, levels):
        coefficients, outgoing = call(
            functools.partial(forward_kernel, level - 1),
            [column_of, sent],
            arrived,
            part,
            blocks,
            perms,
        )
        arrived = swapped(outgoing, "box", level)
        if level == 1:
            narrow_map = ((2 * width, width), thin)
            part, own_map, other_map, sent_map, echo_back = call(
                functools.partial(own_map_kernel, level, last),
                [mixed, ((2 * width, 2 * width), thin), narrow_map, narrow_map, column_of],
                coefficients,
                perms,
                blocks,
                far=(echoes, source_leaf, pulse_slot),
                scratch=[
                    pltpu.VMEM(echoes.shape, thin),
                    pltpu.VMEM(source_leaf.shape, thin),
                    pltpu.VMEM(pulse_slot.shape, jnp.int32),
                    pltpu.SemaphoreType.DMA((2 + scene_chunks,)),
                ],
            )
            arrived_map = swapped(sent_map, "box", last)
        elif level == 2:
            part, echo_part = call(
                functools.partial(own_echo_kernel, level, last),
                [mixed, mixed],
                coefficients,
                perms,
                blocks,
                echo_back,
            )
        elif level < last:
            part = call(
                functools.partial(own_kernel, level), [mixed], coefficients, perms, blocks
            )
    half_wide = ((half, width), wide)
    part, rest, bracket = call(
        functools.partial(bracket_kernel, last),
        [half_wide, half_wide, sent],
        coefficients,
        perms,
        own_map,
        echo_part,
        outgoing,
        arrived_map,
    )
    arrived_bracket = swapped(bracket, "box", last)
    placed = call(
        functools.partial(join_kernel, last), [column_of], arrived, part, other_map, perms
    )
    arrived, more = arrived_bracket, (rest,)
    for level in reversed(range(last)):
        coefficients, outgoing = call(
            functools.partial(backward_kernel, level),
            [column_of, sent],
            arrived,
            placed,
            perms,
            blocks,
            *more,
        )
        arrived, more = swapped(outgoing, "box", level), ()
        placed = call(
            functools.partial(own_back_kernel, level),
            [column_of],
            coefficients,
            blocks,
            perms if level else own_slots,
        )
    return call(
        last_kernel,
        [((rows, samples), thin)],
        arrived,
        placed,
        out_slots,
        leaf_near,
        scene_near,
        far_out=True,
        scratch=[
            pltpu.VMEM((rows, samples), thin),
            pltpu.SemaphoreType.DMA((scene_chunks,)),
        ],
    )


def solution(mesh):
    return jax.shard_map(
        on_device,
        mesh=mesh,
        in_specs=(
            P(("groups", "box"), None),
            P(("groups", "box"), None),
            P(("groups", "box"), None),
            P(("groups", "box"), None),
            P(None, "box", None),
            P(),
            P(),
            P(None, "box", None, None, None),
        ),
        out_specs=P(("groups", "box"), None),
        check_vma=False,
    )
```

```python
import functools

import jax
import jax.numpy as jnp
from jax import lax
from jax.experimental import pallas as pl
from jax.experimental.pallas import tpu as pltpu
from jax.sharding import PartitionSpec as P

step_size = 0.1
wide = jnp.float32
thin = jnp.bfloat16
lanes = 128
depth = 256
scene_chunks = 4


def swapped(value, axis, apart):
    return lax.ppermute(value, axis, [(i, i ^ 1 << apart) for i in range(lax.axis_size(axis))])


def mul(left, right):
    return jnp.dot(left, right, preferred_element_type=wide)


def mul_t(left, right):
    return lax.dot_general(left, right, (((1,), (1,)), ((), ())), preferred_element_type=wide)


def bit_of(level):
    return lax.axis_index("box") // 2**level % 2


def half_row(perm_ref, level, which):
    half = perm_ref.shape[2] // 2
    return perm_ref[level, :, pl.ds(pl.multiple_of(which * half, half), half)]


def column(row):
    parts = []
    for at in range(0, row.shape[1], lanes):
        parts.append(jnp.broadcast_to(row[:, at : at + lanes], (lanes, lanes)).T)
    return jnp.concatenate(parts, axis=0)


def one_hot(hits):
    return jnp.where(hits, 1.0, 0.0).astype(thin)


def fold(slots, half):
    return jnp.where(slots < half, slots, slots - half)


def take(row, both):
    half, width = both.shape[0], both.shape[1] // 2
    slots = column(row)
    within = fold(slots, half)
    lane = lax.broadcasted_iota(jnp.int32, slots.shape, 1)
    total = None
    for at in range(0, half, depth):
        chosen = jnp.concatenate(
            [one_hot(within == lane + (at + more)) for more in range(0, depth, lanes)], axis=1
        )
        part = mul(chosen, both[at : at + depth])
        total = part if total is None else total + part
    return jnp.where(slots < half, total[:, :width], total[:, width:])


def place(row, values, half):
    low = column(row) < half
    values = values.astype(wide)
    zeros = jnp.zeros_like(values)
    spread = jnp.concatenate([jnp.where(low, values, zeros), jnp.where(low, zeros, values)], axis=1)
    spread = spread.astype(thin)
    within = fold(row, half)
    total = None
    target = lax.broadcasted_iota(jnp.int32, (half, depth), 0)
    for at in range(0, values.shape[0], depth):
        chosen = one_hot(target == within[:, at : at + depth])
        part = mul(chosen, spread[at : at + depth])
        total = part if total is None else total + part
    return total


def compose(outer, inner):
    half = outer.shape[1] // 2
    digits = jnp.concatenate([outer // 256, outer % 256], axis=0).astype(wide)
    digits = jnp.concatenate([digits[:, :half], digits[:, half:]], axis=0)
    digits = jnp.pad(digits, ((0, 12), (0, 0))).astype(thin)
    within = fold(inner, half)
    total = None
    target = lax.broadcasted_iota(jnp.int32, (depth, inner.shape[1]), 0)
    for at in range(0, half, depth):
        chosen = one_hot(target + at == within)
        part = mul(digits[:, at : at + depth], chosen)
        total = part if total is None else total + part
    picked = jnp.where(inner < half, total[0:2], total[2:4])
    return (picked[0:1] * 256 + picked[1:2]).astype(jnp.int32)


def stack(values):
    half = values.shape[0] // 2
    return jnp.concatenate([values[:half], values[half:]], axis=1)


def unstack(values):
    width = values.shape[1] // 2
    return jnp.concatenate([values[:, :width], values[:, width:]], axis=0)


def pair_weight(panel_ref, level, which):
    return jnp.concatenate(
        [panel_ref[level, 0, which], panel_ref[level, 0, 2 + which]], axis=1
    )


def pair_weights(panel_ref, level):
    bit = bit_of(level)
    own, other = pair_weight(panel_ref, level, bit), pair_weight(panel_ref, level, 1 - bit)
    return jnp.concatenate([own, other], axis=0)


def first_kernel(
    scene_in, leaf_in, pixel_in, perm_in, panel_in,
    scene_ref, leaf_ref, pixel_ref, perm_ref, panel_ref, leafed_ref, slots_ref, out_ref, done,
):
    rows = scene_ref.shape[0]
    half, width = rows // 2, leaf_ref.shape[1]
    chunk = rows // scene_chunks
    parts = [pl.ds(at * chunk, chunk) for at in range(scene_chunks)]
    pairs = [(pixel_in, pixel_ref), (perm_in, perm_ref), (leaf_in, leaf_ref)]
    pairs += [(scene_in.at[part], scene_ref.at[part]) for part in parts]
    pairs += [(panel_in, panel_ref)]
    loads = [
        pltpu.make_async_copy(source, target, done.at[at])
        for at, (source, target) in enumerate(pairs)
    ]
    for load in loads:
        load.start()
    loads[0].wait()
    loads[1].wait()
    slots = compose(pixel_ref[...], half_row(perm_ref, 0, 1 - bit_of(0)))
    slots_ref[...] = slots
    loads[2].wait()
    for at, part in enumerate(parts):
        loads[3 + at].wait()
        side, first = divmod(at * chunk, half)
        leafed_ref[pl.ds(first, chunk), pl.ds(side * width, width)] = mul(
            scene_ref[part], leaf_ref[...]
        ).astype(thin)
    out_ref[...] = take(slots, leafed_ref[...]).astype(thin)
    loads[-1].wait()


def first_own_kernel(leafed_ref, pixel_ref, perm_ref, panel_ref, slots_ref, part_ref):
    bit = bit_of(0)
    slots = compose(pixel_ref[...], half_row(perm_ref, 0, bit))
    slots_ref[...] = slots
    own = take(slots, leafed_ref[...]).astype(thin)
    part_ref[...] = mul(own, pair_weight(panel_ref, 0, bit))


def own_kernel(level, coef_ref, perm_ref, panel_ref, part_ref):
    bit = bit_of(level)
    own = take(half_row(perm_ref, level, bit), coef_ref[...]).astype(thin)
    part_ref[...] = mul(own, pair_weight(panel_ref, level, bit))


def split(values):
    high = values.astype(thin)
    return jnp.concatenate([high, (values - high.astype(wide)).astype(thin)], axis=0)


def twice(values):
    return jnp.concatenate([values, values], axis=1)


def own_map_kernel(
    level, last, coef_ref, perm_ref, panel_ref, echo_in, leaf_in, slots_in,
    part_ref, own_map_ref, other_map_ref, sent_map_ref, back_ref, echo, leaf, slots, done,
):
    rows = echo.shape[0]
    chunk = rows // scene_chunks
    parts = [pl.ds(at * chunk, chunk) for at in range(scene_chunks)]
    pairs = [(slots_in, slots), (leaf_in, leaf)]
    pairs += [(echo_in.at[part], echo.at[part]) for part in parts]
    loads = [
        pltpu.make_async_copy(source, target, done.at[at])
        for at, (source, target) in enumerate(pairs)
    ]
    for load in loads:
        load.start()
    own_kernel(level, coef_ref, perm_ref, panel_ref, part_ref)
    loads[0].wait()
    loads[1].wait()
    gram = split(mul_t(leaf[...], leaf[...]))
    both = pair_weights(panel_ref, last)
    width = both.shape[0] // 2
    scaled = stack(mul(twice(unstack(both)), gram))
    pair = mul_t(split(scaled), both)
    maps = pair[: 2 * width] + pair[2 * width :]
    own_map_ref[...] = split(maps[:width])
    other_map_ref[...] = split(maps[width:, :width])
    sent_map_ref[...] = split(maps[width:, width:])
    back = []
    for at, part in enumerate(parts):
        loads[2 + at].wait()
        back.append(mul_t(echo[part], leaf[...]).astype(thin))
    back_ref[...] = place(slots[...], jnp.concatenate(back, axis=0), rows // 2).astype(thin)


def own_echo_kernel(
    level, last, coef_ref, perm_ref, panel_ref, back_ref, part_ref, echo_part_ref
):
    own_kernel(level, coef_ref, perm_ref, panel_ref, part_ref)
    echo_part_ref[...] = mul_t(back_ref[...], pair_weights(panel_ref, last))


def mix(level, arrived_ref, part_ref, panel_ref):
    weight = pair_weight(panel_ref, level, 1 - bit_of(level))
    mixture = part_ref[...] + mul(arrived_ref[...], weight)
    return mixture.astype(thin)


def forward_kernel(level, arrived_ref, part_ref, panel_ref, perm_ref, coef_ref, out_ref):
    coefficients = mix(level, arrived_ref, part_ref, panel_ref)
    coef_ref[...] = coefficients
    slots = half_row(perm_ref, level + 1, 1 - bit_of(level + 1))
    out_ref[...] = take(slots, coefficients).astype(thin)


def bracket_kernel(
    level, coef_ref, perm_ref, map_ref, echo_part_ref, sent_ref, arrived_map_ref,
    part_ref, rest_ref, out_ref,
):
    own = take(half_row(perm_ref, level, bit_of(level)), coef_ref[...]).astype(thin)
    both = mul(twice(own), map_ref[...]) - echo_part_ref[...]
    width = own.shape[1]
    part_ref[...] = both[:, :width]
    out_ref[...] = both[:, width:].astype(thin)
    rest_ref[...] = mul(twice(sent_ref[...]), arrived_map_ref[...])


def join_kernel(level, arrived_ref, part_ref, map_ref, perm_ref, placed_ref):
    own = part_ref[...] + mul(twice(arrived_ref[...]), map_ref[...])
    row = half_row(perm_ref, level, bit_of(level))
    placed_ref[...] = place(row, own.astype(thin), placed_ref.shape[0]).astype(thin)


def own_back_kernel(level, coef_ref, panel_ref, perm_ref, placed_ref):
    bit = bit_of(level)
    own = mul_t(coef_ref[...], pair_weight(panel_ref, level, bit)).astype(thin)
    row = half_row(perm_ref, level, bit) if level else perm_ref[...]
    placed_ref[...] = place(row, own, coef_ref.shape[0]).astype(thin)


def backward_kernel(level, arrived_ref, placed_ref, perm_ref, panel_ref, *refs):
    *rest_ref, coef_ref, out_ref = refs
    arrived = arrived_ref[...]
    if rest_ref:
        arrived = (arrived.astype(wide) + rest_ref[0][...]).astype(thin)
    row = half_row(perm_ref, level + 1, 1 - bit_of(level + 1))
    back = place(row, arrived, placed_ref.shape[0]) + placed_ref[...].astype(wide)
    back = back.astype(thin)
    coef_ref[...] = back
    weight = pair_weight(panel_ref, level, 1 - bit_of(level))
    out_ref[...] = mul_t(back, weight).astype(thin)


def last_kernel(arrived_ref, placed_ref, slots_ref, leaf_ref, scene_ref, image_ref, image, sent):
    rows = scene_ref.shape[0]
    chunk = rows // scene_chunks
    back = place(slots_ref[...], arrived_ref[...], rows // 2)
    back = unstack((back + placed_ref[...].astype(wide)).astype(thin))
    stores = []
    for at in range(scene_chunks):
        part = pl.ds(at * chunk, chunk)
        gradient = mul_t(back[at * chunk : (at + 1) * chunk], leaf_ref[...])
        image[part] = (scene_ref[part].astype(wide) - step_size * gradient).astype(thin)
        stores.append(pltpu.make_async_copy(image.at[part], image_ref.at[part], sent.at[at]))
        stores[-1].start()
    for store in stores:
        store.wait()


def call(kernel, outs, *operands, far=(), far_out=False, scratch=()):
    shapes = tuple(jax.ShapeDtypeStruct(shape, kind) for shape, kind in outs)
    near, off = pl.BlockSpec(memory_space=pltpu.VMEM), pl.BlockSpec(memory_space=pltpu.HBM)
    away = tuple(pltpu.with_memory_space_constraint(array, pltpu.HBM) for array in far)
    got = pl.pallas_call(
        kernel,
        out_shape=shapes,
        in_specs=[near] * len(operands) + [off] * len(far),
        out_specs=tuple(off if far_out else near for _ in shapes),
        scratch_shapes=scratch,
        compiler_params=pltpu.CompilerParams(vmem_limit_bytes=16 * 2**20),
        cost_estimate=pl.CostEstimate(flops=10**6, bytes_accessed=10**4, transcendentals=0),
    )(*operands, *away)
    return got[0] if len(outs) == 1 else got


def like(array):
    return (array.shape, array.dtype)


def on_device(
    scene_image, echoes, pixel_slot, pulse_slot, level_perm, target_leaf, source_leaf, panels
):
    levels = lax.axis_size("box").bit_length() - 1
    rows, samples = scene_image.shape
    half = rows // 2
    width = target_leaf.shape[1]
    column_of = ((half, 2 * width), thin)
    row_half = ((1, half), jnp.int32)
    sent = ((half, width), thin)
    mixed = ((half, 2 * width), wide)

    far = (scene_image, target_leaf, pixel_slot, level_perm, panels)
    scene_near, leaf_near, pixel_near, perms, blocks, leafed, out_slots, outgoing = call(
        first_kernel,
        [like(array) for array in far] + [column_of, row_half, sent],
        far=far,
        scratch=[pltpu.SemaphoreType.DMA((4 + scene_chunks,))],
    )
    arrived = swapped(outgoing, "box", 0)
    own_slots, part = call(
        first_own_kernel, [row_half, mixed], leafed, pixel_near, perms, blocks
    )
    last = levels - 1
    for level in range(1, levels):
        coefficients, outgoing = call(
            functools.partial(forward_kernel, level - 1),
            [column_of, sent],
            arrived,
            part,
            blocks,
            perms,
        )
        arrived = swapped(outgoing, "box", level)
        if level == 1:
            narrow_map = ((2 * width, width), thin)
            part, own_map, other_map, sent_map, echo_back = call(
                functools.partial(own_map_kernel, level, last),
                [mixed, ((2 * width, 2 * width), thin), narrow_map, narrow_map, column_of],
                coefficients,
                perms,
                blocks,
                far=(echoes, source_leaf, pulse_slot),
                scratch=[
                    pltpu.VMEM(echoes.shape, thin),
                    pltpu.VMEM(source_leaf.shape, thin),
                    pltpu.VMEM(pulse_slot.shape, jnp.int32),
                    pltpu.SemaphoreType.DMA((2 + scene_chunks,)),
                ],
            )
            arrived_map = swapped(sent_map, "box", last)
        elif level == 2:
            part, echo_part = call(
                functools.partial(own_echo_kernel, level, last),
                [mixed, mixed],
                coefficients,
                perms,
                blocks,
                echo_back,
            )
        elif level < last:
            part = call(
                functools.partial(own_kernel, level), [mixed], coefficients, perms, blocks
            )
    half_wide = ((half, width), wide)
    part, rest, bracket = call(
        functools.partial(bracket_kernel, last),
        [half_wide, half_wide, sent],
        coefficients,
        perms,
        own_map,
        echo_part,
        outgoing,
        arrived_map,
    )
    arrived_bracket = swapped(bracket, "box", last)
    placed = call(
        functools.partial(join_kernel, last), [column_of], arrived, part, other_map, perms
    )
    arrived, more = arrived_bracket, (rest,)
    for level in reversed(range(last)):
        coefficients, outgoing = call(
            functools.partial(backward_kernel, level),
            [column_of, sent],
            arrived,
            placed,
            perms,
            blocks,
            *more,
        )
        arrived, more = swapped(outgoing, "box", level), ()
        placed = call(
            functools.partial(own_back_kernel, level),
            [column_of],
            coefficients,
            blocks,
            perms if level else own_slots,
        )
    return call(
        last_kernel,
        [((rows, samples), thin)],
        arrived,
        placed,
        out_slots,
        leaf_near,
        scene_near,
        far_out=True,
        scratch=[
            pltpu.VMEM((rows, samples), thin),
            pltpu.SemaphoreType.DMA((scene_chunks,)),
        ],
    )


def solution(mesh):
    return jax.shard_map(
        on_device,
        mesh=mesh,
        in_specs=(
            P(("groups", "box"), None),
            P(("groups", "box"), None),
            P(("groups", "box"), None),
            P(("groups", "box"), None),
            P(None, "box", None),
            P(),
            P(),
            P(None, "box", None, None, None),
        ),
        out_specs=P(("groups", "box"), None),
        check_vma=False,
    )
```

```python
import functools

import jax
import jax.numpy as jnp
from jax import lax
from jax.experimental import pallas as pl
from jax.experimental.pallas import tpu as pltpu
from jax.sharding import PartitionSpec as P

step_size = 0.1
wide = jnp.float32
thin = jnp.bfloat16
lanes = 128
scene_chunks = 4


def swapped(value, axis, apart):
    return lax.ppermute(value, axis, [(i, i ^ 1 << apart) for i in range(lax.axis_size(axis))])


def mul(left, right):
    return jnp.dot(left, right, preferred_element_type=wide)


def mul_t(left, right):
    return lax.dot_general(left, right, (((1,), (1,)), ((), ())), preferred_element_type=wide)


def bit_of(level):
    return lax.axis_index("box") // 2**level % 2


def half_row(perm_ref, level, which):
    half = perm_ref.shape[2] // 2
    return perm_ref[level, :, pl.ds(pl.multiple_of(which * half, half), half)]


def column(row):
    parts = []
    for at in range(0, row.shape[1], lanes):
        parts.append(jnp.broadcast_to(row[:, at : at + lanes], (lanes, lanes)).T)
    return jnp.concatenate(parts, axis=0)


def one_hot(hits):
    return jnp.where(hits, 1.0, 0.0).astype(thin)


def fold(slots, half):
    return jnp.where(slots < half, slots, slots - half)


def take_plan(row):
    half = row.shape[1]
    slots = column(row)
    within = fold(slots, half)
    lane = lax.broadcasted_iota(jnp.int32, slots.shape, 1)
    chosen = [one_hot(within == lane + at) for at in range(0, half, lanes)]
    return jnp.concatenate(chosen, axis=1), jnp.where(slots < half, 1.0, 0.0)


def take(plan, both):
    chosen, low = plan
    total = mul(chosen, both)
    width = both.shape[1] // 2
    return jnp.where(low > 0.5, total[:, :width], total[:, width:])


def place_plan(row, half):
    target = lax.broadcasted_iota(jnp.int32, (half, row.shape[1]), 0)
    return one_hot(target == fold(row, half)), one_hot(column(row) < half)


def place(plan, values):
    chosen, low = plan
    return mul(chosen, jnp.concatenate([values * low, values * (1 - low)], axis=1))


def read(refs):
    return tuple(ref[...] for ref in refs)


def write(refs, values):
    for ref, value in zip(refs, values):
        ref[...] = value


def compose(outer, inner):
    half = outer.shape[1] // 2
    digits = jnp.concatenate([outer // 256, outer % 256], axis=0).astype(wide)
    digits = jnp.concatenate([digits[:, :half], digits[:, half:]], axis=0)
    digits = jnp.pad(digits, ((0, 12), (0, 0))).astype(thin)
    target = lax.broadcasted_iota(jnp.int32, (half, inner.shape[1]), 0)
    total = mul(digits, one_hot(target == fold(inner, half)))
    picked = jnp.where(inner < half, total[0:2], total[2:4])
    return (picked[0:1] * 256 + picked[1:2]).astype(jnp.int32)


def stack(values):
    half = values.shape[0] // 2
    return jnp.concatenate([values[:half], values[half:]], axis=1)


def unstack(values):
    width = values.shape[1] // 2
    return jnp.concatenate([values[:, :width], values[:, width:]], axis=0)


def pair_weight(panel_ref, level, which):
    return jnp.concatenate(
        [panel_ref[level, 0, which], panel_ref[level, 0, 2 + which]], axis=1
    )


def pair_weights(panel_ref, level):
    bit = bit_of(level)
    own, other = pair_weight(panel_ref, level, bit), pair_weight(panel_ref, level, 1 - bit)
    return jnp.concatenate([own, other], axis=0)


def first_kernel(
    scene_in, leaf_in, pixel_in, perm_in, panel_in,
    scene_ref, leaf_ref, pixel_ref, perm_ref, panel_ref, leafed_ref, slots_ref, out_ref, done,
):
    rows = scene_ref.shape[0]
    half, width = rows // 2, leaf_ref.shape[1]
    chunk = rows // scene_chunks
    parts = [pl.ds(at * chunk, chunk) for at in range(scene_chunks)]
    pairs = [(pixel_in, pixel_ref), (perm_in, perm_ref), (leaf_in, leaf_ref)]
    pairs += [(scene_in.at[part], scene_ref.at[part]) for part in parts]
    pairs += [(panel_in, panel_ref)]
    loads = [
        pltpu.make_async_copy(source, target, done.at[at])
        for at, (source, target) in enumerate(pairs)
    ]
    for load in loads:
        load.start()
    loads[0].wait()
    loads[1].wait()
    slots = compose(pixel_ref[...], half_row(perm_ref, 0, 1 - bit_of(0)))
    slots_ref[...] = slots
    for load in loads[2:-1]:
        load.wait()
    for at, part in enumerate(parts):
        side, first = divmod(at * chunk, half)
        leafed_ref[pl.ds(first, chunk), pl.ds(side * width, width)] = mul(
            scene_ref[part], leaf_ref[...]
        ).astype(thin)
    out_ref[...] = take(take_plan(slots), leafed_ref[...]).astype(thin)
    loads[-1].wait()


def first_own_kernel(leafed_ref, pixel_ref, perm_ref, panel_ref, slots_ref, part_ref):
    bit = bit_of(0)
    slots = compose(pixel_ref[...], half_row(perm_ref, 0, bit))
    slots_ref[...] = slots
    own = take(take_plan(slots), leafed_ref[...]).astype(thin)
    part_ref[...] = mul(own, pair_weight(panel_ref, 0, bit))


def own_kernel(level, coef_ref, perm_ref, panel_ref, part_ref):
    bit = bit_of(level)
    own = take(take_plan(half_row(perm_ref, level, bit)), coef_ref[...]).astype(thin)
    part_ref[...] = mul(own, pair_weight(panel_ref, level, bit))


def split(values):
    high = values.astype(thin)
    return jnp.concatenate([high, (values - high.astype(wide)).astype(thin)], axis=0)


def twice(values):
    return jnp.concatenate([values, values], axis=1)


def own_map_kernel(
    level, last, coef_ref, perm_ref, panel_ref, echo_in, leaf_in, slots_in,
    part_ref, own_map_ref, other_map_ref, sent_map_ref, back_ref, echo, leaf, slots, done,
):
    rows = echo.shape[0]
    chunk = rows // scene_chunks
    parts = [pl.ds(at * chunk, chunk) for at in range(scene_chunks)]
    pairs = [(slots_in, slots), (leaf_in, leaf)]
    pairs += [(echo_in.at[part], echo.at[part]) for part in parts]
    loads = [
        pltpu.make_async_copy(source, target, done.at[at])
        for at, (source, target) in enumerate(pairs)
    ]
    for load in loads:
        load.start()
    own_kernel(level, coef_ref, perm_ref, panel_ref, part_ref)
    loads[0].wait()
    loads[1].wait()
    gram = split(mul_t(leaf[...], leaf[...]))
    both = pair_weights(panel_ref, last)
    width = both.shape[0] // 2
    scaled = stack(mul(twice(unstack(both)), gram))
    pair = mul_t(split(scaled), both)
    maps = pair[: 2 * width] + pair[2 * width :]
    own_map_ref[...] = split(maps[:width])
    other_map_ref[...] = split(maps[width:, :width])
    sent_map_ref[...] = maps[width:, width:].astype(thin)
    back = []
    for at, part in enumerate(parts):
        loads[2 + at].wait()
        back.append(mul_t(echo[part], leaf[...]).astype(thin))
    plan = place_plan(slots[...], rows // 2)
    back_ref[...] = place(plan, jnp.concatenate(back, axis=0)).astype(thin)


def own_echo_kernel(
    level, last, coef_ref, perm_ref, panel_ref, back_ref, part_ref, echo_part_ref
):
    own_kernel(level, coef_ref, perm_ref, panel_ref, part_ref)
    echo_part_ref[...] = mul_t(back_ref[...], pair_weights(panel_ref, last))


def mix(level, arrived_ref, part_ref, panel_ref):
    weight = pair_weight(panel_ref, level, 1 - bit_of(level))
    mixture = part_ref[...] + mul(arrived_ref[...], weight)
    return mixture.astype(thin)


def forward_kernel(level, arrived_ref, part_ref, panel_ref, perm_ref, coef_ref, out_ref):
    coefficients = mix(level, arrived_ref, part_ref, panel_ref)
    coef_ref[...] = coefficients
    plan = take_plan(half_row(perm_ref, level + 1, 1 - bit_of(level + 1)))
    out_ref[...] = take(plan, coefficients).astype(thin)


def bracket_kernel(
    level, coef_ref, perm_ref, map_ref, echo_part_ref, sent_ref, arrived_map_ref,
    part_ref, rest_ref, out_ref,
):
    plan = take_plan(half_row(perm_ref, level, bit_of(level)))
    own = take(plan, coef_ref[...]).astype(thin)
    both = mul(twice(own), map_ref[...]) - echo_part_ref[...]
    width = own.shape[1]
    part_ref[...] = both[:, :width]
    out_ref[...] = both[:, width:].astype(thin)
    rest_ref[...] = mul(sent_ref[...], arrived_map_ref[...])


def join_kernel(level, arrived_ref, part_ref, map_ref, perm_ref, placed_ref, *plan_refs):
    bit, half = bit_of(level), placed_ref.shape[0]
    own = part_ref[...] + mul(twice(arrived_ref[...]), map_ref[...])
    plan = place_plan(half_row(perm_ref, level, bit), half)
    placed_ref[...] = place(plan, own.astype(thin)).astype(thin)
    write(plan_refs, place_plan(half_row(perm_ref, level, 1 - bit), half))


def own_back_kernel(level, coef_ref, panel_ref, own_ref, other_ref, placed_ref, *plan_refs):
    bit, half = bit_of(level), placed_ref.shape[0]
    own = mul_t(coef_ref[...], pair_weight(panel_ref, level, bit)).astype(thin)
    rows = [own_ref[...], other_ref[...]]
    if level:
        rows = [half_row(own_ref, level, bit), half_row(other_ref, level, 1 - bit)]
    placed_ref[...] = place(place_plan(rows[0], half), own).astype(thin)
    write(plan_refs, place_plan(rows[1], half))


def backward_kernel(
    level, arrived_ref, placed_ref, chosen_ref, low_ref, panel_ref, *refs
):
    *rest_ref, coef_ref, out_ref = refs
    arrived = arrived_ref[...]
    if rest_ref:
        arrived = (arrived.astype(wide) + rest_ref[0][...]).astype(thin)
    back = place(read((chosen_ref, low_ref)), arrived) + placed_ref[...].astype(wide)
    back = back.astype(thin)
    coef_ref[...] = back
    weight = pair_weight(panel_ref, level, 1 - bit_of(level))
    out_ref[...] = mul_t(back, weight).astype(thin)


def last_kernel(
    arrived_ref, placed_ref, chosen_ref, low_ref, leaf_ref, scene_ref, image_ref, image, sent
):
    rows = scene_ref.shape[0]
    chunk = rows // scene_chunks
    back = place(read((chosen_ref, low_ref)), arrived_ref[...])
    back = unstack((back + placed_ref[...].astype(wide)).astype(thin))
    stores = []
    for at in range(scene_chunks):
        part = pl.ds(at * chunk, chunk)
        gradient = mul_t(back[at * chunk : (at + 1) * chunk], leaf_ref[...])
        image[part] = (scene_ref[part].astype(wide) - step_size * gradient).astype(thin)
        stores.append(pltpu.make_async_copy(image.at[part], image_ref.at[part], sent.at[at]))
        stores[-1].start()
    for store in stores:
        store.wait()


def call(kernel, outs, *operands, far=(), far_out=False, scratch=()):
    shapes = tuple(jax.ShapeDtypeStruct(shape, kind) for shape, kind in outs)
    near, off = pl.BlockSpec(memory_space=pltpu.VMEM), pl.BlockSpec(memory_space=pltpu.HBM)
    away = tuple(pltpu.with_memory_space_constraint(array, pltpu.HBM) for array in far)
    got = pl.pallas_call(
        kernel,
        out_shape=shapes,
        in_specs=[near] * len(operands) + [off] * len(far),
        out_specs=tuple(off if far_out else near for _ in shapes),
        scratch_shapes=scratch,
        compiler_params=pltpu.CompilerParams(vmem_limit_bytes=16 * 2**20),
        cost_estimate=pl.CostEstimate(flops=10**6, bytes_accessed=10**4, transcendentals=0),
    )(*operands, *away)
    return got[0] if len(outs) == 1 else got


def like(array):
    return (array.shape, array.dtype)


def on_device(
    scene_image, echoes, pixel_slot, pulse_slot, level_perm, target_leaf, source_leaf, panels
):
    levels = lax.axis_size("box").bit_length() - 1
    rows, samples = scene_image.shape
    half = rows // 2
    width = target_leaf.shape[1]
    column_of = ((half, 2 * width), thin)
    row_half = ((1, half), jnp.int32)
    sent = ((half, width), thin)
    mixed = ((half, 2 * width), wide)

    far = (scene_image, target_leaf, pixel_slot, level_perm, panels)
    scene_near, leaf_near, pixel_near, perms, blocks, leafed, out_slots, outgoing = call(
        first_kernel,
        [like(array) for array in far] + [column_of, row_half, sent],
        far=far,
        scratch=[pltpu.SemaphoreType.DMA((4 + scene_chunks,))],
    )
    arrived = swapped(outgoing, "box", 0)
    place_like = [((half, half), thin), ((half, lanes), thin)]
    own_slots, part = call(
        first_own_kernel, [row_half, mixed], leafed, pixel_near, perms, blocks
    )
    last = levels - 1
    for level in range(1, levels):
        coefficients, outgoing = call(
            functools.partial(forward_kernel, level - 1),
            [column_of, sent],
            arrived,
            part,
            blocks,
            perms,
        )
        arrived = swapped(outgoing, "box", level)
        if level == 1:
            narrow_map = ((2 * width, width), thin)
            part, own_map, other_map, sent_map, echo_back = call(
                functools.partial(own_map_kernel, level, last),
                [mixed, ((2 * width, 2 * width), thin), narrow_map, ((width, width), thin), column_of],
                coefficients,
                perms,
                blocks,
                far=(echoes, source_leaf, pulse_slot),
                scratch=[
                    pltpu.VMEM(echoes.shape, thin),
                    pltpu.VMEM(source_leaf.shape, thin),
                    pltpu.VMEM(pulse_slot.shape, jnp.int32),
                    pltpu.SemaphoreType.DMA((2 + scene_chunks,)),
                ],
            )
            arrived_map = swapped(sent_map, "box", last)
        elif level == 2:
            part, echo_part = call(
                functools.partial(own_echo_kernel, level, last),
                [mixed, mixed],
                coefficients,
                perms,
                blocks,
                echo_back,
            )
        elif level < last:
            part = call(
                functools.partial(own_kernel, level),
                [mixed],
                coefficients,
                perms,
                blocks,
            )
    half_wide = ((half, width), wide)
    part, rest, bracket = call(
        functools.partial(bracket_kernel, last),
        [half_wide, half_wide, sent],
        coefficients,
        perms,
        own_map,
        echo_part,
        outgoing,
        arrived_map,
    )
    arrived_bracket = swapped(bracket, "box", last)
    placed, *plan = call(
        functools.partial(join_kernel, last),
        [column_of] + place_like,
        arrived,
        part,
        other_map,
        perms,
    )
    arrived, more = arrived_bracket, (rest,)
    for level in reversed(range(last)):
        coefficients, outgoing = call(
            functools.partial(backward_kernel, level),
            [column_of, sent],
            arrived,
            placed,
            *plan,
            blocks,
            *more,
        )
        arrived, more = swapped(outgoing, "box", level), ()
        placed, *plan = call(
            functools.partial(own_back_kernel, level),
            [column_of] + place_like,
            coefficients,
            blocks,
            *((perms, perms) if level else (own_slots, out_slots)),
        )
    return call(
        last_kernel,
        [((rows, samples), thin)],
        arrived,
        placed,
        *plan,
        leaf_near,
        scene_near,
        far_out=True,
        scratch=[
            pltpu.VMEM((rows, samples), thin),
            pltpu.SemaphoreType.DMA((scene_chunks,)),
        ],
    )


def solution(mesh):
    return jax.shard_map(
        on_device,
        mesh=mesh,
        in_specs=(
            P(("groups", "box"), None),
            P(("groups", "box"), None),
            P(("groups", "box"), None),
            P(("groups", "box"), None),
            P(None, "box", None),
            P(),
            P(),
            P(None, "box", None, None, None),
        ),
        out_specs=P(("groups", "box"), None),
        check_vma=False,
    )
```

```python
import functools

import jax
import jax.numpy as jnp
from jax import lax
from jax.experimental import pallas as pl
from jax.experimental.pallas import tpu as pltpu
from jax.sharding import PartitionSpec as P

step_size = 0.1
wide = jnp.float32
thin = jnp.bfloat16
lanes = 128
scene_chunks = 4


def swapped(value, axis, apart):
    return lax.ppermute(value, axis, [(i, i ^ 1 << apart) for i in range(lax.axis_size(axis))])


def mul(left, right):
    return jnp.dot(left, right, preferred_element_type=wide)


def mul_t(left, right):
    return lax.dot_general(left, right, (((1,), (1,)), ((), ())), preferred_element_type=wide)


def bit_of(level):
    return lax.axis_index("box") // 2**level % 2


def half_row(perm_ref, level, which):
    half = perm_ref.shape[2] // 2
    return perm_ref[level, :, pl.ds(pl.multiple_of(which * half, half), half)]


def column(row):
    parts = []
    for at in range(0, row.shape[1], lanes):
        parts.append(jnp.broadcast_to(row[:, at : at + lanes], (lanes, lanes)).T)
    return jnp.concatenate(parts, axis=0)


def one_hot(hits):
    return jnp.where(hits, 1.0, 0.0).astype(thin)


def fold(slots, half):
    return jnp.where(slots < half, slots, slots - half)


def take_plan(row):
    half = row.shape[1]
    slots = column(row)
    within = fold(slots, half)
    lane = lax.broadcasted_iota(jnp.int32, slots.shape, 1)
    chosen = [one_hot(within == lane + at) for at in range(0, half, lanes)]
    return jnp.concatenate(chosen, axis=1), jnp.where(slots < half, 1.0, 0.0)


def take(plan, both):
    chosen, low = plan
    total = mul(chosen, both)
    width = both.shape[1] // 2
    return jnp.where(low > 0.5, total[:, :width], total[:, width:])


def place_plan(row, half):
    target = lax.broadcasted_iota(jnp.int32, (half, row.shape[1]), 0)
    return one_hot(target == fold(row, half)), one_hot(column(row) < half)


def place(plan, values):
    chosen, low = plan
    return mul(chosen, jnp.concatenate([values * low, values * (1 - low)], axis=1))


def compose(outer, inner):
    half = outer.shape[1] // 2
    digits = jnp.concatenate([outer // 256, outer % 256], axis=0).astype(wide)
    digits = jnp.concatenate([digits[:, :half], digits[:, half:]], axis=0)
    digits = jnp.pad(digits, ((0, 12), (0, 0))).astype(thin)
    target = lax.broadcasted_iota(jnp.int32, (half, inner.shape[1]), 0)
    total = mul(digits, one_hot(target == fold(inner, half)))
    picked = jnp.where(inner < half, total[0:2], total[2:4])
    return (picked[0:1] * 256 + picked[1:2]).astype(jnp.int32)


def stack(values):
    half = values.shape[0] // 2
    return jnp.concatenate([values[:half], values[half:]], axis=1)


def unstack(values):
    width = values.shape[1] // 2
    return jnp.concatenate([values[:, :width], values[:, width:]], axis=0)


def pair_weight(panel_ref, level, which):
    return jnp.concatenate(
        [panel_ref[level, 0, which], panel_ref[level, 0, 2 + which]], axis=1
    )


def pair_weights(panel_ref, level):
    bit = bit_of(level)
    own, other = pair_weight(panel_ref, level, bit), pair_weight(panel_ref, level, 1 - bit)
    return jnp.concatenate([own, other], axis=0)


def first_kernel(
    scene_in, leaf_in, pixel_in, perm_in, panel_in,
    scene_ref, leaf_ref, pixel_ref, perm_ref, panel_ref, leafed_ref, slots_ref, out_ref, done,
):
    rows = scene_ref.shape[0]
    half, width = rows // 2, leaf_ref.shape[1]
    chunk = rows // scene_chunks
    parts = [pl.ds(at * chunk, chunk) for at in range(scene_chunks)]
    pairs = [(pixel_in, pixel_ref), (perm_in, perm_ref), (leaf_in, leaf_ref)]
    pairs += [(scene_in.at[part], scene_ref.at[part]) for part in parts]
    pairs += [(panel_in, panel_ref)]
    loads = [
        pltpu.make_async_copy(source, target, done.at[at])
        for at, (source, target) in enumerate(pairs)
    ]
    for load in loads:
        load.start()
    loads[0].wait()
    loads[1].wait()
    slots = compose(pixel_ref[...], half_row(perm_ref, 0, 1 - bit_of(0)))
    slots_ref[...] = slots
    for load in loads[2:-1]:
        load.wait()
    for at, part in enumerate(parts):
        side, first = divmod(at * chunk, half)
        leafed_ref[pl.ds(first, chunk), pl.ds(side * width, width)] = mul(
            scene_ref[part], leaf_ref[...]
        ).astype(thin)
    out_ref[...] = take(take_plan(slots), leafed_ref[...]).astype(thin)
    loads[-1].wait()


def first_own_kernel(leafed_ref, pixel_ref, perm_ref, panel_ref, slots_ref, part_ref):
    bit = bit_of(0)
    slots = compose(pixel_ref[...], half_row(perm_ref, 0, bit))
    slots_ref[...] = slots
    own = take(take_plan(slots), leafed_ref[...]).astype(thin)
    part_ref[...] = mul(own, pair_weight(panel_ref, 0, bit))


def own_kernel(level, coef_ref, perm_ref, panel_ref, part_ref):
    bit = bit_of(level)
    own = take(take_plan(half_row(perm_ref, level, bit)), coef_ref[...]).astype(thin)
    part_ref[...] = mul(own, pair_weight(panel_ref, level, bit))


def split(values):
    high = values.astype(thin)
    return jnp.concatenate([high, (values - high.astype(wide)).astype(thin)], axis=0)


def twice(values):
    return jnp.concatenate([values, values], axis=1)


def echo_loads(echo_in, leaf_in, slots_in, echo, leaf, slots, done):
    rows = echo.shape[0]
    chunk = rows // scene_chunks
    parts = [pl.ds(at * chunk, chunk) for at in range(scene_chunks)]
    pairs = [(slots_in, slots), (leaf_in, leaf)]
    pairs += [(echo_in.at[part], echo.at[part]) for part in parts]
    return [
        pltpu.make_async_copy(source, target, done.at[at])
        for at, (source, target) in enumerate(pairs)
    ]


def echo_back(loads, echo, leaf, slots, back_ref):
    half = echo.shape[0] // 2
    chunk = echo.shape[0] // scene_chunks
    loads[0].wait()
    plan = place_plan(slots[...], half)
    loads[1].wait()
    back = []
    for at in range(scene_chunks):
        loads[2 + at].wait()
        back.append(mul_t(echo[pl.ds(at * chunk, chunk)], leaf[...]).astype(thin))
    back_ref[...] = place(plan, jnp.concatenate(back, axis=0)).astype(thin)


def own_map_kernel(
    level, last, coef_ref, perm_ref, panel_ref, echo_in, leaf_in, slots_in,
    part_ref, own_map_ref, other_map_ref, sent_map_ref, back_ref, echo, leaf, slots, done,
):
    loads = echo_loads(echo_in, leaf_in, slots_in, echo, leaf, slots, done)
    early = bit_of(0) == 0

    @pl.when(early)
    def _():
        for load in loads:
            load.start()

    @pl.when(jnp.logical_not(early))
    def _():
        loads[1].start()
        loads[1].wait()

    own_kernel(level, coef_ref, perm_ref, panel_ref, part_ref)

    @pl.when(early)
    def _():
        echo_back(loads, echo, leaf, slots, back_ref)

    gram = split(mul_t(leaf[...], leaf[...]))
    both = pair_weights(panel_ref, last)
    width = both.shape[0] // 2
    scaled = stack(mul(twice(unstack(both)), gram))
    pair = mul_t(split(scaled), both)
    maps = pair[: 2 * width] + pair[2 * width :]
    own_map_ref[...] = split(maps[:width])
    other_map_ref[...] = split(maps[width:, :width])
    sent_map_ref[...] = maps[width:, width:].astype(thin)


def mix(level, arrived_ref, part_ref, panel_ref):
    weight = pair_weight(panel_ref, level, 1 - bit_of(level))
    mixture = part_ref[...] + mul(arrived_ref[...], weight)
    return mixture.astype(thin)


def forward_kernel(level, arrived_ref, part_ref, panel_ref, perm_ref, coef_ref, out_ref):
    coefficients = mix(level, arrived_ref, part_ref, panel_ref)
    coef_ref[...] = coefficients
    plan = take_plan(half_row(perm_ref, level + 1, 1 - bit_of(level + 1)))
    out_ref[...] = take(plan, coefficients).astype(thin)


def own_echo_kernel(
    level, last, coef_ref, perm_ref, panel_ref, back_ref, part_ref, echo_part_ref
):
    own_kernel(level, coef_ref, perm_ref, panel_ref, part_ref)

    @pl.when(bit_of(0) == 0)
    def _():
        echo_part_ref[...] = mul_t(back_ref[...], pair_weights(panel_ref, last))


def make_plans(perm_ref, slots_refs, chosen_ref, low_ref):
    half = chosen_ref.shape[1]
    for level in range(perm_ref.shape[0]):
        bit = bit_of(level)
        for side in range(2):
            row = half_row(perm_ref, level, bit if side == 0 else 1 - bit)
            if level == 0:
                row = slots_refs[side][...]
            chosen_ref[2 * level + side], low_ref[2 * level + side] = place_plan(row, half)


def bracket_kernel(
    level, coef_ref, perm_ref, map_ref, panel_ref, early_ref, own_slots_ref, out_slots_ref,
    sent_ref, arrived_map_ref, echo_in, leaf_in, slots_in,
    part_ref, rest_ref, out_ref, chosen_ref, low_ref, echo_part_ref, back_ref, echo, leaf, slots, done,
):
    loads = echo_loads(echo_in, leaf_in, slots_in, echo, leaf, slots, done)
    early = bit_of(0) == 0

    @pl.when(early)
    def _():
        echo_part_ref[...] = early_ref[...]

    @pl.when(jnp.logical_not(early))
    def _():
        for load in loads:
            load.start()
        make_plans(perm_ref, (own_slots_ref, out_slots_ref), chosen_ref, low_ref)
        echo_back(loads, echo, leaf, slots, back_ref)
        echo_part_ref[...] = mul_t(back_ref[...], pair_weights(panel_ref, level))

    plan = take_plan(half_row(perm_ref, level, bit_of(level)))
    own = take(plan, coef_ref[...]).astype(thin)
    both = mul(twice(own), map_ref[...]) - echo_part_ref[...]
    width = own.shape[1]
    part_ref[...] = both[:, :width]
    out_ref[...] = both[:, width:].astype(thin)
    rest_ref[...] = mul(sent_ref[...], arrived_map_ref[...])


def plan_kernel(
    perm_ref, own_slots_ref, out_slots_ref, chosen_in, low_in, chosen_ref, low_ref
):
    del chosen_in, low_in

    @pl.when(bit_of(0) == 0)
    def _():
        make_plans(perm_ref, (own_slots_ref, out_slots_ref), chosen_ref, low_ref)


def planned(level, side, chosen_ref, low_ref):
    return chosen_ref[2 * level + side], low_ref[2 * level + side]


def join_kernel(level, arrived_ref, part_ref, map_ref, chosen_ref, low_ref, placed_ref):
    own = part_ref[...] + mul(twice(arrived_ref[...]), map_ref[...])
    plan = planned(level, 0, chosen_ref, low_ref)
    placed_ref[...] = place(plan, own.astype(thin)).astype(thin)


def own_back_kernel(level, coef_ref, panel_ref, chosen_ref, low_ref, placed_ref):
    own = mul_t(coef_ref[...], pair_weight(panel_ref, level, bit_of(level))).astype(thin)
    plan = planned(level, 0, chosen_ref, low_ref)
    placed_ref[...] = place(plan, own).astype(thin)


def backward_kernel(level, arrived_ref, placed_ref, chosen_ref, low_ref, panel_ref, *refs):
    *rest_ref, coef_ref, out_ref = refs
    arrived = arrived_ref[...]
    if rest_ref:
        arrived = (arrived.astype(wide) + rest_ref[0][...]).astype(thin)
    plan = planned(level + 1, 1, chosen_ref, low_ref)
    back = place(plan, arrived) + placed_ref[...].astype(wide)
    back = back.astype(thin)
    coef_ref[...] = back
    weight = pair_weight(panel_ref, level, 1 - bit_of(level))
    out_ref[...] = mul_t(back, weight).astype(thin)


def last_kernel(
    arrived_ref, placed_ref, chosen_ref, low_ref, leaf_ref, scene_ref, image_ref, image, sent
):
    rows = scene_ref.shape[0]
    chunk = rows // scene_chunks
    back = place(planned(0, 1, chosen_ref, low_ref), arrived_ref[...])
    back = unstack((back + placed_ref[...].astype(wide)).astype(thin))
    stores = []
    for at in range(scene_chunks):
        part = pl.ds(at * chunk, chunk)
        gradient = mul_t(back[at * chunk : (at + 1) * chunk], leaf_ref[...])
        image[part] = (scene_ref[part].astype(wide) - step_size * gradient).astype(thin)
        stores.append(pltpu.make_async_copy(image.at[part], image_ref.at[part], sent.at[at]))
        stores[-1].start()
    for store in stores:
        store.wait()


def call(kernel, outs, *operands, far=(), far_out=False, scratch=(), aliases={}):
    shapes = tuple(jax.ShapeDtypeStruct(shape, kind) for shape, kind in outs)
    near, off = pl.BlockSpec(memory_space=pltpu.VMEM), pl.BlockSpec(memory_space=pltpu.HBM)
    away = tuple(pltpu.with_memory_space_constraint(array, pltpu.HBM) for array in far)
    got = pl.pallas_call(
        kernel,
        out_shape=shapes,
        in_specs=[near] * len(operands) + [off] * len(far),
        out_specs=tuple(off if far_out else near for _ in shapes),
        scratch_shapes=scratch,
        input_output_aliases=aliases,
        compiler_params=pltpu.CompilerParams(vmem_limit_bytes=16 * 2**20),
        cost_estimate=pl.CostEstimate(flops=10**6, bytes_accessed=10**4, transcendentals=0),
    )(*operands, *away)
    return got[0] if len(outs) == 1 else got


def like(array):
    return (array.shape, array.dtype)


def on_device(
    scene_image, echoes, pixel_slot, pulse_slot, level_perm, target_leaf, source_leaf, panels
):
    levels = lax.axis_size("box").bit_length() - 1
    rows, samples = scene_image.shape
    half = rows // 2
    width = target_leaf.shape[1]
    column_of = ((half, 2 * width), thin)
    row_half = ((1, half), jnp.int32)
    sent = ((half, width), thin)
    mixed = ((half, 2 * width), wide)

    far = (scene_image, target_leaf, pixel_slot, level_perm, panels)
    scene_near, leaf_near, pixel_near, perms, blocks, leafed, out_slots, outgoing = call(
        first_kernel,
        [like(array) for array in far] + [column_of, row_half, sent],
        far=far,
        scratch=[pltpu.SemaphoreType.DMA((4 + scene_chunks,))],
    )
    arrived = swapped(outgoing, "box", 0)
    place_like = [((half, half), thin), ((half, lanes), thin)]
    own_slots, part = call(
        first_own_kernel, [row_half, mixed], leafed, pixel_near, perms, blocks
    )
    last = levels - 1
    echo_scratch = [
        pltpu.VMEM(echoes.shape, thin),
        pltpu.VMEM(source_leaf.shape, thin),
        pltpu.VMEM(pulse_slot.shape, jnp.int32),
        pltpu.SemaphoreType.DMA((2 + scene_chunks,)),
    ]
    for level in range(1, levels):
        coefficients, outgoing = call(
            functools.partial(forward_kernel, level - 1),
            [column_of, sent],
            arrived,
            part,
            blocks,
            perms,
        )
        arrived = swapped(outgoing, "box", level)
        if level == 1:
            narrow_map = ((2 * width, width), thin)
            part, own_map, other_map, sent_map, early = call(
                functools.partial(own_map_kernel, level, last),
                [mixed, ((2 * width, 2 * width), thin), narrow_map, ((width, width), thin), column_of],
                coefficients,
                perms,
                blocks,
                far=(echoes, source_leaf, pulse_slot),
                scratch=echo_scratch,
            )
            arrived_map = swapped(sent_map, "box", last)
        elif level == 2:
            part, early = call(
                functools.partial(own_echo_kernel, level, last),
                [mixed, mixed],
                coefficients,
                perms,
                blocks,
                early,
            )
        elif level < last:
            part = call(
                functools.partial(own_kernel, level),
                [mixed],
                coefficients,
                perms,
                blocks,
            )
    half_wide = ((half, width), wide)
    plan_like = [((2 * levels, half, half), thin), ((2 * levels, half, lanes), thin)]
    part, rest, bracket, *plans = call(
        functools.partial(bracket_kernel, last),
        [half_wide, half_wide, sent] + plan_like,
        coefficients,
        perms,
        own_map,
        blocks,
        early,
        own_slots,
        out_slots,
        outgoing,
        arrived_map,
        far=(echoes, source_leaf, pulse_slot),
        scratch=[pltpu.VMEM((half, 2 * width), wide), pltpu.VMEM((half, 2 * width), thin)]
        + echo_scratch,
    )
    arrived_bracket = swapped(bracket, "box", last)
    plans = call(
        plan_kernel, plan_like, perms, own_slots, out_slots, *plans, aliases={3: 0, 4: 1}
    )
    placed = call(
        functools.partial(join_kernel, last), [column_of], arrived, part, other_map, *plans
    )
    arrived, more = arrived_bracket, (rest,)
    for level in reversed(range(last)):
        coefficients, outgoing = call(
            functools.partial(backward_kernel, level),
            [column_of, sent],
            arrived,
            placed,
            *plans,
            blocks,
            *more,
        )
        arrived, more = swapped(outgoing, "box", level), ()
        placed = call(
            functools.partial(own_back_kernel, level), [column_of], coefficients, blocks, *plans
        )
    return call(
        last_kernel,
        [((rows, samples), thin)],
        arrived,
        placed,
        *plans,
        leaf_near,
        scene_near,
        far_out=True,
        scratch=[
            pltpu.VMEM((rows, samples), thin),
            pltpu.SemaphoreType.DMA((scene_chunks,)),
        ],
    )


def solution(mesh):
    return jax.shard_map(
        on_device,
        mesh=mesh,
        in_specs=(
            P(("groups", "box"), None),
            P(("groups", "box"), None),
            P(("groups", "box"), None),
            P(("groups", "box"), None),
            P(None, "box", None),
            P(),
            P(),
            P(None, "box", None, None, None),
        ),
        out_specs=P(("groups", "box"), None),
        check_vma=False,
    )
```

```python
import functools

import jax
import jax.numpy as jnp
from jax import lax
from jax.experimental import pallas as pl
from jax.experimental.pallas import tpu as pltpu
from jax.sharding import PartitionSpec as P

step_size = 0.1
wide = jnp.float32
thin = jnp.bfloat16
lanes = 128
scene_chunks = 4


def swapped(value, axis, apart):
    return lax.ppermute(value, axis, [(i, i ^ 1 << apart) for i in range(lax.axis_size(axis))])


def mul(left, right):
    return jnp.dot(left, right, preferred_element_type=wide)


def mul_t(left, right):
    return lax.dot_general(left, right, (((1,), (1,)), ((), ())), preferred_element_type=wide)


def bit_of(level):
    return lax.axis_index("box") // 2**level % 2


def half_row(perm_ref, level, which):
    half = perm_ref.shape[2] // 2
    return perm_ref[level, :, pl.ds(pl.multiple_of(which * half, half), half)]


def column(row):
    parts = []
    for at in range(0, row.shape[1], lanes):
        parts.append(jnp.broadcast_to(row[:, at : at + lanes], (lanes, lanes)).T)
    return jnp.concatenate(parts, axis=0)


def one_hot(hits):
    return jnp.where(hits, 1.0, 0.0).astype(thin)


def fold(slots, half):
    return jnp.where(slots < half, slots, slots - half)


def take_plan(row):
    half = row.shape[1]
    slots = column(row)
    within = fold(slots, half)
    lane = lax.broadcasted_iota(jnp.int32, slots.shape, 1)
    chosen = [one_hot(within == lane + at) for at in range(0, half, lanes)]
    return jnp.concatenate(chosen, axis=1), jnp.where(slots < half, 1.0, 0.0)


def take(plan, both):
    chosen, low = plan
    total = mul(chosen, both)
    width = both.shape[1] // 2
    return jnp.where(low > 0.5, total[:, :width], total[:, width:])


def place_plan(row, half):
    target = lax.broadcasted_iota(jnp.int32, (half, row.shape[1]), 0)
    return one_hot(target == fold(row, half)), one_hot(column(row) < half)


def place(plan, values):
    chosen, low = plan
    return mul(chosen, jnp.concatenate([values * low, values * (1 - low)], axis=1))


def compose(outer, inner):
    half = outer.shape[1] // 2
    digits = jnp.concatenate([outer // 256, outer % 256], axis=0).astype(wide)
    digits = jnp.concatenate([digits[:, :half], digits[:, half:]], axis=0)
    digits = jnp.pad(digits, ((0, 12), (0, 0))).astype(thin)
    target = lax.broadcasted_iota(jnp.int32, (half, inner.shape[1]), 0)
    total = mul(digits, one_hot(target == fold(inner, half)))
    picked = jnp.where(inner < half, total[0:2], total[2:4])
    return (picked[0:1] * 256 + picked[1:2]).astype(jnp.int32)


def stack(values):
    half = values.shape[0] // 2
    return jnp.concatenate([values[:half], values[half:]], axis=1)


def unstack(values):
    width = values.shape[1] // 2
    return jnp.concatenate([values[:, :width], values[:, width:]], axis=0)


def pair_weight(panel_ref, level, which):
    return jnp.concatenate(
        [panel_ref[level, 0, which], panel_ref[level, 0, 2 + which]], axis=1
    )


def pair_weights(panel_ref, level):
    bit = bit_of(level)
    own, other = pair_weight(panel_ref, level, bit), pair_weight(panel_ref, level, 1 - bit)
    return jnp.concatenate([own, other], axis=0)


def first_kernel(
    scene_in, leaf_in, pixel_in, perm_in, panel_in,
    scene_ref, leaf_ref, pixel_ref, perm_ref, panel_ref, leafed_ref, slots_ref, out_ref, done,
):
    rows = scene_ref.shape[0]
    half, width = rows // 2, leaf_ref.shape[1]
    chunk = rows // scene_chunks
    parts = [pl.ds(at * chunk, chunk) for at in range(scene_chunks)]
    pairs = [(pixel_in, pixel_ref), (perm_in, perm_ref), (leaf_in, leaf_ref)]
    pairs += [(scene_in.at[part], scene_ref.at[part]) for part in parts]
    pairs += [(panel_in, panel_ref)]
    loads = [
        pltpu.make_async_copy(source, target, done.at[at])
        for at, (source, target) in enumerate(pairs)
    ]
    for at in (0, 1, 2, 3, 5, 4, 6, 7):
        loads[at].start()
    loads[0].wait()
    loads[1].wait()
    slots = compose(pixel_ref[...], half_row(perm_ref, 0, 1 - bit_of(0)))
    slots_ref[...] = slots
    loads[2].wait()
    chosen, low = take_plan(slots)
    total = None
    for at in range(0, half, chunk):
        loads[3 + at // chunk].wait()
        loads[3 + (half + at) // chunk].wait()
        pieces = [
            mul(scene_ref[pl.ds(side * half + at, chunk)], leaf_ref[...]).astype(thin)
            for side in range(2)
        ]
        both = jnp.concatenate(pieces, axis=1)
        leafed_ref[pl.ds(at, chunk)] = both
        piece = mul(chosen[:, at : at + chunk], both)
        total = piece if total is None else total + piece
    out_ref[...] = jnp.where(low > 0.5, total[:, :width], total[:, width:]).astype(thin)
    loads[-1].wait()


def first_own_kernel(leafed_ref, pixel_ref, perm_ref, panel_ref, slots_ref, part_ref):
    bit = bit_of(0)
    slots = compose(pixel_ref[...], half_row(perm_ref, 0, bit))
    slots_ref[...] = slots
    own = take(take_plan(slots), leafed_ref[...]).astype(thin)
    part_ref[...] = mul(own, pair_weight(panel_ref, 0, bit))


def own_kernel(level, coef_ref, perm_ref, panel_ref, part_ref):
    bit = bit_of(level)
    own = take(take_plan(half_row(perm_ref, level, bit)), coef_ref[...]).astype(thin)
    part_ref[...] = mul(own, pair_weight(panel_ref, level, bit))


def split(values):
    high = values.astype(thin)
    return jnp.concatenate([high, (values - high.astype(wide)).astype(thin)], axis=0)


def twice(values):
    return jnp.concatenate([values, values], axis=1)


def echo_loads(echo_in, leaf_in, slots_in, echo, leaf, slots, done):
    rows = echo.shape[0]
    chunk = rows // scene_chunks
    parts = [pl.ds(at * chunk, chunk) for at in range(scene_chunks)]
    pairs = [(slots_in, slots), (leaf_in, leaf)]
    pairs += [(echo_in.at[part], echo.at[part]) for part in parts]
    return [
        pltpu.make_async_copy(source, target, done.at[at])
        for at, (source, target) in enumerate(pairs)
    ]


def echo_back(loads, echo, leaf, slots, back_ref, turns):
    half = echo.shape[0] // 2
    chunk = echo.shape[0] // scene_chunks
    loads[0].wait()
    plan = place_plan(slots[...], half)
    loads[1].wait()
    back = []
    for turn in turns or (range(scene_chunks),):
        for at in turn if turns else ():
            loads[2 + at].start()
        for at in turn:
            loads[2 + at].wait()
            back.append(mul_t(echo[pl.ds(at * chunk, chunk)], leaf[...]).astype(thin))
    back_ref[...] = place(plan, jnp.concatenate(back, axis=0)).astype(thin)


def own_map_kernel(
    level, last, coef_ref, perm_ref, panel_ref, echo_in, leaf_in, slots_in,
    part_ref, own_map_ref, other_map_ref, sent_map_ref, back_ref, echo, leaf, slots, done,
):
    loads = echo_loads(echo_in, leaf_in, slots_in, echo, leaf, slots, done)
    early = bit_of(0) == 0

    @pl.when(early)
    def _():
        for load in loads:
            load.start()

    @pl.when(jnp.logical_not(early))
    def _():
        loads[1].start()
        loads[1].wait()

    own_kernel(level, coef_ref, perm_ref, panel_ref, part_ref)

    @pl.when(early)
    def _():
        echo_back(loads, echo, leaf, slots, back_ref, None)

    gram = split(mul_t(leaf[...], leaf[...]))
    both = pair_weights(panel_ref, last)
    width = both.shape[0] // 2
    scaled = stack(mul(twice(unstack(both)), gram))
    pair = mul_t(split(scaled), both)
    maps = pair[: 2 * width] + pair[2 * width :]
    own_map_ref[...] = split(maps[:width])
    other_map_ref[...] = split(maps[width:, :width])
    sent_map_ref[...] = maps[width:, width:].astype(thin)


def mix(level, arrived_ref, part_ref, panel_ref):
    weight = pair_weight(panel_ref, level, 1 - bit_of(level))
    mixture = part_ref[...] + mul(arrived_ref[...], weight)
    return mixture.astype(thin)


def forward_kernel(level, arrived_ref, part_ref, panel_ref, perm_ref, coef_ref, out_ref):
    weight = pair_weight(panel_ref, level, 1 - bit_of(level))
    chosen, low = take_plan(half_row(perm_ref, level + 1, 1 - bit_of(level + 1)))
    half, width = arrived_ref.shape
    step = half // 2
    total = None
    for at in range(0, half, step):
        part = pl.ds(at, step)
        mixture = (part_ref[part] + mul(arrived_ref[part], weight)).astype(thin)
        coef_ref[part] = mixture
        piece = mul(chosen[:, at : at + step], mixture)
        total = piece if total is None else total + piece
    out_ref[...] = jnp.where(low > 0.5, total[:, :width], total[:, width:]).astype(thin)


def own_echo_kernel(
    level, last, coef_ref, perm_ref, panel_ref, back_ref, part_ref, echo_part_ref
):
    own_kernel(level, coef_ref, perm_ref, panel_ref, part_ref)

    @pl.when(bit_of(0) == 0)
    def _():
        echo_part_ref[...] = mul_t(back_ref[...], pair_weights(panel_ref, last))


def make_plans(perm_ref, slots_refs, chosen_ref, low_ref):
    half = chosen_ref.shape[1]
    for level in range(perm_ref.shape[0]):
        bit = bit_of(level)
        for side in range(2):
            row = half_row(perm_ref, level, bit if side == 0 else 1 - bit)
            if level == 0:
                row = slots_refs[side][...]
            chosen_ref[2 * level + side], low_ref[2 * level + side] = place_plan(row, half)


def bracket_kernel(
    level, coef_ref, perm_ref, map_ref, panel_ref, early_ref, own_slots_ref, out_slots_ref,
    sent_ref, arrived_map_ref, echo_in, leaf_in, slots_in,
    part_ref, rest_ref, out_ref, chosen_ref, low_ref, echo_part_ref, back_ref, echo, leaf, slots, done,
):
    loads = echo_loads(echo_in, leaf_in, slots_in, echo, leaf, slots, done)
    early = bit_of(0) == 0

    @pl.when(early)
    def _():
        echo_part_ref[...] = early_ref[...]

    @pl.when(jnp.logical_not(early))
    def _():
        for load in loads[:2]:
            load.start()
        make_plans(perm_ref, (own_slots_ref, out_slots_ref), chosen_ref, low_ref)
        echo_back(loads, echo, leaf, slots, back_ref, ((0,), (1,), (2, 3)))
        echo_part_ref[...] = mul_t(back_ref[...], pair_weights(panel_ref, level))

    plan = take_plan(half_row(perm_ref, level, bit_of(level)))
    own = take(plan, coef_ref[...]).astype(thin)
    both = mul(twice(own), map_ref[...]) - echo_part_ref[...]
    width = own.shape[1]
    part_ref[...] = both[:, :width]
    out_ref[...] = both[:, width:].astype(thin)
    rest_ref[...] = mul(sent_ref[...], arrived_map_ref[...])


def plan_kernel(
    perm_ref, own_slots_ref, out_slots_ref, chosen_in, low_in, chosen_ref, low_ref
):
    del chosen_in, low_in

    @pl.when(bit_of(0) == 0)
    def _():
        make_plans(perm_ref, (own_slots_ref, out_slots_ref), chosen_ref, low_ref)


def planned(level, side, chosen_ref, low_ref):
    return chosen_ref[2 * level + side], low_ref[2 * level + side]


def join_kernel(level, arrived_ref, part_ref, map_ref, chosen_ref, low_ref, placed_ref):
    own = part_ref[...] + mul(twice(arrived_ref[...]), map_ref[...])
    plan = planned(level, 0, chosen_ref, low_ref)
    placed_ref[...] = place(plan, own.astype(thin)).astype(thin)


def own_back_kernel(level, coef_ref, panel_ref, chosen_ref, low_ref, placed_ref):
    own = mul_t(coef_ref[...], pair_weight(panel_ref, level, bit_of(level))).astype(thin)
    plan = planned(level, 0, chosen_ref, low_ref)
    placed_ref[...] = place(plan, own).astype(thin)


def backward_kernel(level, arrived_ref, placed_ref, chosen_ref, low_ref, panel_ref, *refs):
    *rest_ref, coef_ref, out_ref = refs
    arrived = arrived_ref[...]
    if rest_ref:
        arrived = (arrived.astype(wide) + rest_ref[0][...]).astype(thin)
    plan = planned(level + 1, 1, chosen_ref, low_ref)
    back = place(plan, arrived) + placed_ref[...].astype(wide)
    back = back.astype(thin)
    coef_ref[...] = back
    weight = pair_weight(panel_ref, level, 1 - bit_of(level))
    out_ref[...] = mul_t(back, weight).astype(thin)


def last_kernel(
    arrived_ref, placed_ref, chosen_ref, low_ref, leaf_ref, scene_ref, image_ref, image, sent
):
    rows = scene_ref.shape[0]
    chunk = rows // scene_chunks
    back = place(planned(0, 1, chosen_ref, low_ref), arrived_ref[...])
    back = unstack((back + placed_ref[...].astype(wide)).astype(thin))
    stores = []
    for at in range(scene_chunks):
        part = pl.ds(at * chunk, chunk)
        gradient = mul_t(back[at * chunk : (at + 1) * chunk], leaf_ref[...])
        image[part] = (scene_ref[part].astype(wide) - step_size * gradient).astype(thin)
        stores.append(pltpu.make_async_copy(image.at[part], image_ref.at[part], sent.at[at]))
        stores[-1].start()
    for store in stores:
        store.wait()


def call(kernel, outs, *operands, far=(), far_out=False, scratch=(), aliases={}):
    shapes = tuple(jax.ShapeDtypeStruct(shape, kind) for shape, kind in outs)
    near, off = pl.BlockSpec(memory_space=pltpu.VMEM), pl.BlockSpec(memory_space=pltpu.HBM)
    away = tuple(pltpu.with_memory_space_constraint(array, pltpu.HBM) for array in far)
    got = pl.pallas_call(
        kernel,
        out_shape=shapes,
        in_specs=[near] * len(operands) + [off] * len(far),
        out_specs=tuple(off if far_out else near for _ in shapes),
        scratch_shapes=scratch,
        input_output_aliases=aliases,
        compiler_params=pltpu.CompilerParams(vmem_limit_bytes=16 * 2**20),
        cost_estimate=pl.CostEstimate(flops=10**6, bytes_accessed=10**4, transcendentals=0),
    )(*operands, *away)
    return got[0] if len(outs) == 1 else got


def like(array):
    return (array.shape, array.dtype)


def on_device(
    scene_image, echoes, pixel_slot, pulse_slot, level_perm, target_leaf, source_leaf, panels
):
    levels = lax.axis_size("box").bit_length() - 1
    rows, samples = scene_image.shape
    half = rows // 2
    width = target_leaf.shape[1]
    column_of = ((half, 2 * width), thin)
    row_half = ((1, half), jnp.int32)
    sent = ((half, width), thin)
    mixed = ((half, 2 * width), wide)

    far = (scene_image, target_leaf, pixel_slot, level_perm, panels)
    scene_near, leaf_near, pixel_near, perms, blocks, leafed, out_slots, outgoing = call(
        first_kernel,
        [like(array) for array in far] + [column_of, row_half, sent],
        far=far,
        scratch=[pltpu.SemaphoreType.DMA((4 + scene_chunks,))],
    )
    arrived = swapped(outgoing, "box", 0)
    place_like = [((half, half), thin), ((half, lanes), thin)]
    own_slots, part = call(
        first_own_kernel, [row_half, mixed], leafed, pixel_near, perms, blocks
    )
    last = levels - 1
    echo_scratch = [
        pltpu.VMEM(echoes.shape, thin),
        pltpu.VMEM(source_leaf.shape, thin),
        pltpu.VMEM(pulse_slot.shape, jnp.int32),
        pltpu.SemaphoreType.DMA((2 + scene_chunks,)),
    ]
    for level in range(1, levels):
        coefficients, outgoing = call(
            functools.partial(forward_kernel, level - 1),
            [column_of, sent],
            arrived,
            part,
            blocks,
            perms,
        )
        arrived = swapped(outgoing, "box", level)
        if level == 1:
            narrow_map = ((2 * width, width), thin)
            part, own_map, other_map, sent_map, early = call(
                functools.partial(own_map_kernel, level, last),
                [mixed, ((2 * width, 2 * width), thin), narrow_map, ((width, width), thin), column_of],
                coefficients,
                perms,
                blocks,
                far=(echoes, source_leaf, pulse_slot),
                scratch=echo_scratch,
            )
            arrived_map = swapped(sent_map, "box", last)
        elif level == 2:
            part, early = call(
                functools.partial(own_echo_kernel, level, last),
                [mixed, mixed],
                coefficients,
                perms,
                blocks,
                early,
            )
        elif level < last:
            part = call(
                functools.partial(own_kernel, level),
                [mixed],
                coefficients,
                perms,
                blocks,
            )
    half_wide = ((half, width), wide)
    plan_like = [((2 * levels, half, half), thin), ((2 * levels, half, lanes), thin)]
    part, rest, bracket, *plans = call(
        functools.partial(bracket_kernel, last),
        [half_wide, half_wide, sent] + plan_like,
        coefficients,
        perms,
        own_map,
        blocks,
        early,
        own_slots,
        out_slots,
        outgoing,
        arrived_map,
        far=(echoes, source_leaf, pulse_slot),
        scratch=[pltpu.VMEM((half, 2 * width), wide), pltpu.VMEM((half, 2 * width), thin)]
        + echo_scratch,
    )
    arrived_bracket = swapped(bracket, "box", last)
    plans = call(
        plan_kernel, plan_like, perms, own_slots, out_slots, *plans, aliases={3: 0, 4: 1}
    )
    placed = call(
        functools.partial(join_kernel, last), [column_of], arrived, part, other_map, *plans
    )
    arrived, more = arrived_bracket, (rest,)
    for level in reversed(range(last)):
        coefficients, outgoing = call(
            functools.partial(backward_kernel, level),
            [column_of, sent],
            arrived,
            placed,
            *plans,
            blocks,
            *more,
        )
        arrived, more = swapped(outgoing, "box", level), ()
        placed = call(
            functools.partial(own_back_kernel, level), [column_of], coefficients, blocks, *plans
        )
    return call(
        last_kernel,
        [((rows, samples), thin)],
        arrived,
        placed,
        *plans,
        leaf_near,
        scene_near,
        far_out=True,
        scratch=[
            pltpu.VMEM((rows, samples), thin),
            pltpu.SemaphoreType.DMA((scene_chunks,)),
        ],
    )


def solution(mesh):
    return jax.shard_map(
        on_device,
        mesh=mesh,
        in_specs=(
            P(("groups", "box"), None),
            P(("groups", "box"), None),
            P(("groups", "box"), None),
            P(("groups", "box"), None),
            P(None, "box", None),
            P(),
            P(),
            P(None, "box", None, None, None),
        ),
        out_specs=P(("groups", "box"), None),
        check_vma=False,
    )
```

```python
import functools

import jax
import jax.numpy as jnp
from jax import lax
from jax.experimental import pallas as pl
from jax.experimental.pallas import tpu as pltpu
from jax.sharding import PartitionSpec as P

step_size = 0.1
wide = jnp.float32
thin = jnp.bfloat16
lanes = 128
scene_chunks = 4


def swapped(value, axis, apart):
    return lax.ppermute(value, axis, [(i, i ^ 1 << apart) for i in range(lax.axis_size(axis))])


def mul(left, right):
    return jnp.dot(left, right, preferred_element_type=wide)


def mul_t(left, right):
    return lax.dot_general(left, right, (((1,), (1,)), ((), ())), preferred_element_type=wide)


def bit_of(level):
    return lax.axis_index("box") // 2**level % 2


def half_row(perm_ref, level, which):
    half = perm_ref.shape[2] // 2
    return perm_ref[level, :, pl.ds(pl.multiple_of(which * half, half), half)]


def column(row):
    parts = []
    for at in range(0, row.shape[1], lanes):
        parts.append(jnp.broadcast_to(row[:, at : at + lanes], (lanes, lanes)).T)
    return jnp.concatenate(parts, axis=0)


def one_hot(hits):
    return jnp.where(hits, 1.0, 0.0).astype(thin)


def fold(slots, half):
    return jnp.where(slots < half, slots, slots - half)


def take_plan(row):
    half = row.shape[1]
    slots = column(row)
    within = fold(slots, half)
    lane = lax.broadcasted_iota(jnp.int32, slots.shape, 1)
    chosen = [one_hot(within == lane + at) for at in range(0, half, lanes)]
    return jnp.concatenate(chosen, axis=1), jnp.where(slots < half, 1.0, 0.0)


def take(plan, both):
    chosen, low = plan
    total = mul(chosen, both)
    width = both.shape[1] // 2
    return jnp.where(low > 0.5, total[:, :width], total[:, width:])


def place_plan(row, half):
    target = lax.broadcasted_iota(jnp.int32, (half, row.shape[1]), 0)
    return one_hot(target == fold(row, half)), one_hot(column(row) < half)


def place(plan, values):
    chosen, low = plan
    return mul(chosen, jnp.concatenate([values * low, values * (1 - low)], axis=1))


def compose(outer, inner):
    half = outer.shape[1] // 2
    digits = jnp.concatenate([outer // 256, outer % 256], axis=0).astype(wide)
    digits = jnp.concatenate([digits[:, :half], digits[:, half:]], axis=0)
    digits = jnp.pad(digits, ((0, 12), (0, 0))).astype(thin)
    target = lax.broadcasted_iota(jnp.int32, (half, inner.shape[1]), 0)
    total = mul(digits, one_hot(target == fold(inner, half)))
    picked = jnp.where(inner < half, total[0:2], total[2:4])
    return (picked[0:1] * 256 + picked[1:2]).astype(jnp.int32)


def stack(values):
    half = values.shape[0] // 2
    return jnp.concatenate([values[:half], values[half:]], axis=1)


def unstack(values):
    width = values.shape[1] // 2
    return jnp.concatenate([values[:, :width], values[:, width:]], axis=0)


def pair_weight(panel_ref, level, which):
    return jnp.concatenate(
        [panel_ref[level, 0, which], panel_ref[level, 0, 2 + which]], axis=1
    )


def pair_weights(panel_ref, level):
    bit = bit_of(level)
    own, other = pair_weight(panel_ref, level, bit), pair_weight(panel_ref, level, 1 - bit)
    return jnp.concatenate([own, other], axis=0)


def first_kernel(
    scene_in, leaf_in, pixel_in, perm_in, panel_in,
    scene_ref, leaf_ref, pixel_ref, perm_ref, panel_ref, leafed_ref, slots_ref, out_ref, done,
):
    rows = scene_ref.shape[0]
    half, width = rows // 2, leaf_ref.shape[1]
    chunk = rows // scene_chunks
    parts = [pl.ds(at * chunk, chunk) for at in range(scene_chunks)]
    pairs = [(pixel_in, pixel_ref), (perm_in, perm_ref), (leaf_in, leaf_ref)]
    pairs += [(scene_in.at[part], scene_ref.at[part]) for part in parts]
    pairs += [(panel_in, panel_ref)]
    loads = [
        pltpu.make_async_copy(source, target, done.at[at])
        for at, (source, target) in enumerate(pairs)
    ]
    for at in (0, 1, 2, 3, 5, 4, 6, 7):
        loads[at].start()
    loads[0].wait()
    loads[1].wait()
    slots = compose(pixel_ref[...], half_row(perm_ref, 0, 1 - bit_of(0)))
    slots_ref[...] = slots
    loads[2].wait()
    chosen, low = take_plan(slots)
    total = None
    for at in range(0, half, chunk):
        loads[3 + at // chunk].wait()
        loads[3 + (half + at) // chunk].wait()
        pieces = [
            mul(scene_ref[pl.ds(side * half + at, chunk)], leaf_ref[...]).astype(thin)
            for side in range(2)
        ]
        both = jnp.concatenate(pieces, axis=1)
        leafed_ref[pl.ds(at, chunk)] = both
        piece = mul(chosen[:, at : at + chunk], both)
        total = piece if total is None else total + piece
    out_ref[...] = jnp.where(low > 0.5, total[:, :width], total[:, width:]).astype(thin)
    loads[-1].wait()


def first_own_kernel(leafed_ref, pixel_ref, perm_ref, panel_ref, slots_ref, part_ref):
    bit = bit_of(0)
    slots = compose(pixel_ref[...], half_row(perm_ref, 0, bit))
    slots_ref[...] = slots
    own = take(take_plan(slots), leafed_ref[...]).astype(thin)
    part_ref[...] = mul(own, pair_weight(panel_ref, 0, bit))


def own_kernel(level, coef_ref, perm_ref, panel_ref, part_ref):
    bit = bit_of(level)
    own = take(take_plan(half_row(perm_ref, level, bit)), coef_ref[...]).astype(thin)
    part_ref[...] = mul(own, pair_weight(panel_ref, level, bit))


def split(values):
    high = values.astype(thin)
    return jnp.concatenate([high, (values - high.astype(wide)).astype(thin)], axis=0)


def twice(values):
    return jnp.concatenate([values, values], axis=1)


def echo_loads(echo_in, leaf_in, slots_in, echo, leaf, slots, done):
    rows = echo.shape[0]
    chunk = rows // scene_chunks
    parts = [pl.ds(at * chunk, chunk) for at in range(scene_chunks)]
    pairs = [(slots_in, slots), (leaf_in, leaf)]
    pairs += [(echo_in.at[part], echo.at[part]) for part in parts]
    return [
        pltpu.make_async_copy(source, target, done.at[at])
        for at, (source, target) in enumerate(pairs)
    ]


def echo_back(loads, echo, leaf, slots, back_ref, turns):
    half = echo.shape[0] // 2
    chunk = echo.shape[0] // scene_chunks
    loads[0].wait()
    plan = place_plan(slots[...], half)
    loads[1].wait()
    back = []
    for turn in turns or (range(scene_chunks),):
        for at in turn if turns else ():
            loads[2 + at].start()
        for at in turn:
            loads[2 + at].wait()
            back.append(mul_t(echo[pl.ds(at * chunk, chunk)], leaf[...]).astype(thin))
    back_ref[...] = place(plan, jnp.concatenate(back, axis=0)).astype(thin)


def own_map_kernel(
    level, last, coef_ref, perm_ref, panel_ref, echo_in, leaf_in, slots_in,
    part_ref, own_map_ref, other_map_ref, sent_map_ref, back_ref, echo, leaf, slots, done,
):
    loads = echo_loads(echo_in, leaf_in, slots_in, echo, leaf, slots, done)
    early = bit_of(0) == 0

    @pl.when(early)
    def _():
        for load in loads:
            load.start()

    @pl.when(jnp.logical_not(early))
    def _():
        loads[1].start()
        loads[1].wait()

    own_kernel(level, coef_ref, perm_ref, panel_ref, part_ref)

    @pl.when(early)
    def _():
        echo_back(loads, echo, leaf, slots, back_ref, None)

    gram = split(mul_t(leaf[...], leaf[...]))
    both = pair_weights(panel_ref, last)
    width = both.shape[0] // 2
    scaled = stack(mul(twice(unstack(both)), gram))
    pair = mul_t(split(scaled), both)
    maps = pair[: 2 * width] + pair[2 * width :]
    own_map_ref[...] = split(maps[:width])
    other_map_ref[...] = split(maps[width:, :width])
    sent_map_ref[...] = maps[width:, width:].astype(thin)


def mix(level, arrived_ref, part_ref, panel_ref):
    weight = pair_weight(panel_ref, level, 1 - bit_of(level))
    mixture = part_ref[...] + mul(arrived_ref[...], weight)
    return mixture.astype(thin)


def forward_kernel(level, arrived_ref, part_ref, panel_ref, perm_ref, coef_ref, out_ref):
    weight = pair_weight(panel_ref, level, 1 - bit_of(level))
    chosen, low = take_plan(half_row(perm_ref, level + 1, 1 - bit_of(level + 1)))
    half, width = arrived_ref.shape
    step = half // 2
    total = None
    for at in range(0, half, step):
        part = pl.ds(at, step)
        mixture = (part_ref[part] + mul(arrived_ref[part], weight)).astype(thin)
        coef_ref[part] = mixture
        piece = mul(chosen[:, at : at + step], mixture)
        total = piece if total is None else total + piece
    out_ref[...] = jnp.where(low > 0.5, total[:, :width], total[:, width:]).astype(thin)


def own_echo_kernel(
    level, last, coef_ref, perm_ref, panel_ref, back_ref, part_ref, echo_part_ref
):
    own_kernel(level, coef_ref, perm_ref, panel_ref, part_ref)

    @pl.when(bit_of(0) == 0)
    def _():
        echo_part_ref[...] = mul_t(back_ref[...], pair_weights(panel_ref, last))


def make_plans(perm_ref, slots_refs, chosen_ref, low_ref):
    half = chosen_ref.shape[1]
    for level in range(perm_ref.shape[0]):
        bit = bit_of(level)
        for side in range(2):
            row = half_row(perm_ref, level, bit if side == 0 else 1 - bit)
            if level == 0:
                row = slots_refs[side][...]
            chosen_ref[2 * level + side], low_ref[2 * level + side] = place_plan(row, half)


def bracket_kernel(
    level, coef_ref, perm_ref, map_ref, panel_ref, early_ref, own_slots_ref, out_slots_ref,
    arrived_map_ref, echo_in, leaf_in, slots_in,
    part_ref, kept_map_ref, out_ref, chosen_ref, low_ref, echo_part_ref, back_ref,
    echo, leaf, slots, done,
):
    loads = echo_loads(echo_in, leaf_in, slots_in, echo, leaf, slots, done)
    early = bit_of(0) == 0

    @pl.when(early)
    def _():
        echo_part_ref[...] = early_ref[...]

    @pl.when(jnp.logical_not(early))
    def _():
        for load in loads[:2]:
            load.start()
        make_plans(perm_ref, (own_slots_ref, out_slots_ref), chosen_ref, low_ref)
        echo_back(loads, echo, leaf, slots, back_ref, ((0,), (1,), (2, 3)))
        echo_part_ref[...] = mul_t(back_ref[...], pair_weights(panel_ref, level))

    plan = take_plan(half_row(perm_ref, level, bit_of(level)))
    own = take(plan, coef_ref[...]).astype(thin)
    both = mul(twice(own), map_ref[...]) - echo_part_ref[...]
    width = own.shape[1]
    part_ref[...] = both[:, :width]
    out_ref[...] = both[:, width:].astype(thin)
    kept_map_ref[...] = arrived_map_ref[...]


def plan_kernel(
    perm_ref, own_slots_ref, out_slots_ref, chosen_in, low_in, sent_ref, map_ref,
    chosen_ref, low_ref, rest_ref,
):
    del chosen_in, low_in
    rest_ref[...] = mul(sent_ref[...], map_ref[...])

    @pl.when(bit_of(0) == 0)
    def _():
        make_plans(perm_ref, (own_slots_ref, out_slots_ref), chosen_ref, low_ref)


def planned(level, side, chosen_ref, low_ref):
    return chosen_ref[2 * level + side], low_ref[2 * level + side]


def join_kernel(level, arrived_ref, part_ref, map_ref, chosen_ref, low_ref, placed_ref):
    own = part_ref[...] + mul(twice(arrived_ref[...]), map_ref[...])
    plan = planned(level, 0, chosen_ref, low_ref)
    placed_ref[...] = place(plan, own.astype(thin)).astype(thin)


def own_back_kernel(level, coef_ref, panel_ref, chosen_ref, low_ref, placed_ref):
    own = mul_t(coef_ref[...], pair_weight(panel_ref, level, bit_of(level))).astype(thin)
    plan = planned(level, 0, chosen_ref, low_ref)
    placed_ref[...] = place(plan, own).astype(thin)


def backward_kernel(level, arrived_ref, placed_ref, chosen_ref, low_ref, panel_ref, *refs):
    *rest_ref, coef_ref, out_ref = refs
    arrived = arrived_ref[...]
    if rest_ref:
        arrived = (arrived.astype(wide) + rest_ref[0][...]).astype(thin)
    plan = planned(level + 1, 1, chosen_ref, low_ref)
    back = place(plan, arrived) + placed_ref[...].astype(wide)
    back = back.astype(thin)
    coef_ref[...] = back
    weight = pair_weight(panel_ref, level, 1 - bit_of(level))
    out_ref[...] = mul_t(back, weight).astype(thin)


def last_kernel(
    arrived_ref, placed_ref, chosen_ref, low_ref, leaf_ref, scene_ref, image_ref, image, sent
):
    rows = scene_ref.shape[0]
    chunk = rows // scene_chunks
    back = place(planned(0, 1, chosen_ref, low_ref), arrived_ref[...])
    back = unstack((back + placed_ref[...].astype(wide)).astype(thin))
    stores = []
    for at in range(scene_chunks):
        part = pl.ds(at * chunk, chunk)
        gradient = mul_t(back[at * chunk : (at + 1) * chunk], leaf_ref[...])
        image[part] = (scene_ref[part].astype(wide) - step_size * gradient).astype(thin)
        stores.append(pltpu.make_async_copy(image.at[part], image_ref.at[part], sent.at[at]))
        stores[-1].start()
    for store in stores:
        store.wait()


def call(kernel, outs, *operands, far=(), far_out=False, scratch=(), aliases={}):
    shapes = tuple(jax.ShapeDtypeStruct(shape, kind) for shape, kind in outs)
    near, off = pl.BlockSpec(memory_space=pltpu.VMEM), pl.BlockSpec(memory_space=pltpu.HBM)
    away = tuple(pltpu.with_memory_space_constraint(array, pltpu.HBM) for array in far)
    got = pl.pallas_call(
        kernel,
        out_shape=shapes,
        in_specs=[near] * len(operands) + [off] * len(far),
        out_specs=tuple(off if far_out else near for _ in shapes),
        scratch_shapes=scratch,
        input_output_aliases=aliases,
        compiler_params=pltpu.CompilerParams(vmem_limit_bytes=16 * 2**20),
        cost_estimate=pl.CostEstimate(flops=10**6, bytes_accessed=10**4, transcendentals=0),
    )(*operands, *away)
    return got[0] if len(outs) == 1 else got


def like(array):
    return (array.shape, array.dtype)


def on_device(
    scene_image, echoes, pixel_slot, pulse_slot, level_perm, target_leaf, source_leaf, panels
):
    levels = lax.axis_size("box").bit_length() - 1
    rows, samples = scene_image.shape
    half = rows // 2
    width = target_leaf.shape[1]
    column_of = ((half, 2 * width), thin)
    row_half = ((1, half), jnp.int32)
    sent = ((half, width), thin)
    mixed = ((half, 2 * width), wide)

    far = (scene_image, target_leaf, pixel_slot, level_perm, panels)
    scene_near, leaf_near, pixel_near, perms, blocks, leafed, out_slots, outgoing = call(
        first_kernel,
        [like(array) for array in far] + [column_of, row_half, sent],
        far=far,
        scratch=[pltpu.SemaphoreType.DMA((4 + scene_chunks,))],
    )
    arrived = swapped(outgoing, "box", 0)
    place_like = [((half, half), thin), ((half, lanes), thin)]
    own_slots, part = call(
        first_own_kernel, [row_half, mixed], leafed, pixel_near, perms, blocks
    )
    last = levels - 1
    echo_scratch = [
        pltpu.VMEM(echoes.shape, thin),
        pltpu.VMEM(source_leaf.shape, thin),
        pltpu.VMEM(pulse_slot.shape, jnp.int32),
        pltpu.SemaphoreType.DMA((2 + scene_chunks,)),
    ]
    for level in range(1, levels):
        coefficients, outgoing = call(
            functools.partial(forward_kernel, level - 1),
            [column_of, sent],
            arrived,
            part,
            blocks,
            perms,
        )
        arrived = swapped(outgoing, "box", level)
        if level == 1:
            narrow_map = ((2 * width, width), thin)
            part, own_map, other_map, sent_map, early = call(
                functools.partial(own_map_kernel, level, last),
                [mixed, ((2 * width, 2 * width), thin), narrow_map, ((width, width), thin), column_of],
                coefficients,
                perms,
                blocks,
                far=(echoes, source_leaf, pulse_slot),
                scratch=echo_scratch,
            )
            arrived_map = swapped(sent_map, "box", last)
        elif level == 2:
            part, early = call(
                functools.partial(own_echo_kernel, level, last),
                [mixed, mixed],
                coefficients,
                perms,
                blocks,
                early,
            )
        elif level < last:
            part = call(
                functools.partial(own_kernel, level),
                [mixed],
                coefficients,
                perms,
                blocks,
            )
    half_wide = ((half, width), wide)
    plan_like = [((2 * levels, half, half), thin), ((2 * levels, half, lanes), thin)]
    part, arrived_map, bracket, *plans = call(
        functools.partial(bracket_kernel, last),
        [half_wide, ((width, width), thin), sent] + plan_like,
        coefficients,
        perms,
        own_map,
        blocks,
        early,
        own_slots,
        out_slots,
        arrived_map,
        far=(echoes, source_leaf, pulse_slot),
        scratch=[pltpu.VMEM((half, 2 * width), wide), pltpu.VMEM((half, 2 * width), thin)]
        + echo_scratch,
    )
    arrived_bracket = swapped(bracket, "box", last)
    *plans, rest = call(
        plan_kernel,
        plan_like + [half_wide],
        perms,
        own_slots,
        out_slots,
        *plans,
        outgoing,
        arrived_map,
        aliases={3: 0, 4: 1},
    )
    placed = call(
        functools.partial(join_kernel, last), [column_of], arrived, part, other_map, *plans
    )
    arrived, more = arrived_bracket, (rest,)
    for level in reversed(range(last)):
        coefficients, outgoing = call(
            functools.partial(backward_kernel, level),
            [column_of, sent],
            arrived,
            placed,
            *plans,
            blocks,
            *more,
        )
        arrived, more = swapped(outgoing, "box", level), ()
        placed = call(
            functools.partial(own_back_kernel, level), [column_of], coefficients, blocks, *plans
        )
    return call(
        last_kernel,
        [((rows, samples), thin)],
        arrived,
        placed,
        *plans,
        leaf_near,
        scene_near,
        far_out=True,
        scratch=[
            pltpu.VMEM((rows, samples), thin),
            pltpu.SemaphoreType.DMA((scene_chunks,)),
        ],
    )


def solution(mesh):
    return jax.shard_map(
        on_device,
        mesh=mesh,
        in_specs=(
            P(("groups", "box"), None),
            P(("groups", "box"), None),
            P(("groups", "box"), None),
            P(("groups", "box"), None),
            P(None, "box", None),
            P(),
            P(),
            P(None, "box", None, None, None),
        ),
        out_specs=P(("groups", "box"), None),
        check_vma=False,
    )
```

```python
import functools

import jax
import jax.numpy as jnp
from jax import lax
from jax.experimental import pallas as pl
from jax.experimental.pallas import tpu as pltpu
from jax.sharding import PartitionSpec as P

step_size = 0.1
wide = jnp.float32
thin = jnp.bfloat16
lanes = 128
scene_chunks = 4


def swapped(value, axis, apart):
    return lax.ppermute(value, axis, [(i, i ^ 1 << apart) for i in range(lax.axis_size(axis))])


def mul(left, right):
    return jnp.dot(left, right, preferred_element_type=wide)


def mul_t(left, right):
    return lax.dot_general(left, right, (((1,), (1,)), ((), ())), preferred_element_type=wide)


def bit_of(level):
    return lax.axis_index("box") // 2**level % 2


def half_row(perm_ref, level, which):
    half = perm_ref.shape[2] // 2
    return perm_ref[level, :, pl.ds(pl.multiple_of(which * half, half), half)]


def column(row):
    parts = []
    for at in range(0, row.shape[1], lanes):
        parts.append(jnp.broadcast_to(row[:, at : at + lanes], (lanes, lanes)).T)
    return jnp.concatenate(parts, axis=0)


def one_hot(hits):
    return jnp.where(hits, 1.0, 0.0).astype(thin)


def fold(slots, half):
    return jnp.where(slots < half, slots, slots - half)


def take_plan(row):
    half = row.shape[1]
    slots = column(row)
    within = fold(slots, half)
    lane = lax.broadcasted_iota(jnp.int32, slots.shape, 1)
    chosen = [one_hot(within == lane + at) for at in range(0, half, lanes)]
    return jnp.concatenate(chosen, axis=1), jnp.where(slots < half, 1.0, 0.0)


def take(plan, both):
    chosen, low = plan
    total = mul(chosen, both)
    width = both.shape[1] // 2
    return jnp.where(low > 0.5, total[:, :width], total[:, width:])


def place_plan(row, half):
    target = lax.broadcasted_iota(jnp.int32, (half, row.shape[1]), 0)
    return one_hot(target == fold(row, half)), one_hot(column(row) < half)


def place(plan, values):
    chosen, low = plan
    return mul(chosen, jnp.concatenate([values * low, values * (1 - low)], axis=1))


def compose(outer, inner):
    half = outer.shape[1] // 2
    digits = jnp.concatenate([outer // 256, outer % 256], axis=0).astype(wide)
    digits = jnp.concatenate([digits[:, :half], digits[:, half:]], axis=0)
    digits = jnp.pad(digits, ((0, 12), (0, 0))).astype(thin)
    target = lax.broadcasted_iota(jnp.int32, (half, inner.shape[1]), 0)
    total = mul(digits, one_hot(target == fold(inner, half)))
    picked = jnp.where(inner < half, total[0:2], total[2:4])
    return (picked[0:1] * 256 + picked[1:2]).astype(jnp.int32)


def stack(values):
    half = values.shape[0] // 2
    return jnp.concatenate([values[:half], values[half:]], axis=1)


def unstack(values):
    width = values.shape[1] // 2
    return jnp.concatenate([values[:, :width], values[:, width:]], axis=0)


def pair_weight(panel_ref, level, which):
    return jnp.concatenate(
        [panel_ref[level, 0, which], panel_ref[level, 0, 2 + which]], axis=1
    )


def pair_weights(panel_ref, level):
    bit = bit_of(level)
    own, other = pair_weight(panel_ref, level, bit), pair_weight(panel_ref, level, 1 - bit)
    return jnp.concatenate([own, other], axis=0)


def first_kernel(
    scene_in, leaf_in, pixel_in, perm_in, panel_in,
    scene_ref, leaf_ref, pixel_ref, perm_ref, panel_ref, leafed_ref, slots_ref, out_ref, done,
):
    rows = scene_ref.shape[0]
    half, width = rows // 2, leaf_ref.shape[1]
    chunk = rows // scene_chunks
    parts = [pl.ds(at * chunk, chunk) for at in range(scene_chunks)]
    pairs = [(pixel_in, pixel_ref), (perm_in, perm_ref), (leaf_in, leaf_ref)]
    pairs += [(scene_in.at[part], scene_ref.at[part]) for part in parts]
    pairs += [(panel_in, panel_ref)]
    loads = [
        pltpu.make_async_copy(source, target, done.at[at])
        for at, (source, target) in enumerate(pairs)
    ]
    for at in (0, 1, 2, 3, 5, 4, 6, 7):
        loads[at].start()
    loads[0].wait()
    loads[1].wait()
    slots = compose(pixel_ref[...], half_row(perm_ref, 0, 1 - bit_of(0)))
    slots_ref[...] = slots
    chosen, low = take_plan(slots)
    loads[2].wait()
    total = None
    for at in range(0, half, chunk):
        loads[3 + at // chunk].wait()
        loads[3 + (half + at) // chunk].wait()
        pieces = [
            mul(scene_ref[pl.ds(side * half + at, chunk)], leaf_ref[...]).astype(thin)
            for side in range(2)
        ]
        both = jnp.concatenate(pieces, axis=1)
        leafed_ref[pl.ds(at, chunk)] = both
        piece = mul(chosen[:, at : at + chunk], both)
        total = piece if total is None else total + piece
    out_ref[...] = jnp.where(low > 0.5, total[:, :width], total[:, width:]).astype(thin)
    loads[-1].wait()


def first_own_kernel(leafed_ref, pixel_ref, perm_ref, panel_ref, slots_ref, part_ref):
    bit = bit_of(0)
    slots = compose(pixel_ref[...], half_row(perm_ref, 0, bit))
    slots_ref[...] = slots
    own = take(take_plan(slots), leafed_ref[...]).astype(thin)
    part_ref[...] = mul(own, pair_weight(panel_ref, 0, bit))


def own_kernel(level, coef_ref, perm_ref, panel_ref, part_ref):
    bit = bit_of(level)
    own = take(take_plan(half_row(perm_ref, level, bit)), coef_ref[...]).astype(thin)
    part_ref[...] = mul(own, pair_weight(panel_ref, level, bit))


def split(values):
    high = values.astype(thin)
    return jnp.concatenate([high, (values - high.astype(wide)).astype(thin)], axis=0)


def twice(values):
    return jnp.concatenate([values, values], axis=1)


def echo_loads(echo_in, leaf_in, slots_in, echo, leaf, slots, done):
    rows = echo.shape[0]
    chunk = rows // scene_chunks
    parts = [pl.ds(at * chunk, chunk) for at in range(scene_chunks)]
    pairs = [(slots_in, slots), (leaf_in, leaf)]
    pairs += [(echo_in.at[part], echo.at[part]) for part in parts]
    return [
        pltpu.make_async_copy(source, target, done.at[at])
        for at, (source, target) in enumerate(pairs)
    ]


def echo_back(loads, echo, leaf, slots, back_ref, turns):
    half = echo.shape[0] // 2
    chunk = echo.shape[0] // scene_chunks
    for at in turns[0] if turns else ():
        loads[2 + at].start()
    loads[0].wait()
    plan = place_plan(slots[...], half)
    loads[1].wait()
    back = []
    for turn in turns or (range(scene_chunks),):
        for at in turn if turns and turn != turns[0] else ():
            loads[2 + at].start()
        for at in turn:
            loads[2 + at].wait()
            back.append(mul_t(echo[pl.ds(at * chunk, chunk)], leaf[...]).astype(thin))
    back_ref[...] = place(plan, jnp.concatenate(back, axis=0)).astype(thin)


def own_map_kernel(
    level, last, coef_ref, perm_ref, panel_ref, echo_in, leaf_in, slots_in,
    part_ref, own_map_ref, other_map_ref, sent_map_ref, back_ref, echo, leaf, slots, done,
):
    loads = echo_loads(echo_in, leaf_in, slots_in, echo, leaf, slots, done)
    early = bit_of(0) == 0

    @pl.when(early)
    def _():
        for load in loads:
            load.start()

    @pl.when(jnp.logical_not(early))
    def _():
        loads[1].start()
        loads[1].wait()

    own_kernel(level, coef_ref, perm_ref, panel_ref, part_ref)

    @pl.when(early)
    def _():
        echo_back(loads, echo, leaf, slots, back_ref, None)

    gram = split(mul_t(leaf[...], leaf[...]))
    both = pair_weights(panel_ref, last)
    width = both.shape[0] // 2
    scaled = stack(mul(twice(unstack(both)), gram))
    pair = mul_t(split(scaled), both)
    maps = pair[: 2 * width] + pair[2 * width :]
    own_map_ref[...] = split(maps[:width])
    other_map_ref[...] = split(maps[width:, :width])
    sent_map_ref[...] = maps[width:, width:].astype(thin)


def mix(level, arrived_ref, part_ref, panel_ref):
    weight = pair_weight(panel_ref, level, 1 - bit_of(level))
    mixture = part_ref[...] + mul(arrived_ref[...], weight)
    return mixture.astype(thin)


def forward_kernel(level, arrived_ref, part_ref, panel_ref, perm_ref, coef_ref, out_ref):
    weight = pair_weight(panel_ref, level, 1 - bit_of(level))
    chosen, low = take_plan(half_row(perm_ref, level + 1, 1 - bit_of(level + 1)))
    half, width = arrived_ref.shape
    step = half // 2
    total = None
    for at in range(0, half, step):
        part = pl.ds(at, step)
        mixture = (part_ref[part] + mul(arrived_ref[part], weight)).astype(thin)
        coef_ref[part] = mixture
        piece = mul(chosen[:, at : at + step], mixture)
        total = piece if total is None else total + piece
    out_ref[...] = jnp.where(low > 0.5, total[:, :width], total[:, width:]).astype(thin)


def own_echo_kernel(
    level, last, coef_ref, perm_ref, panel_ref, back_ref, part_ref, echo_part_ref
):
    own_kernel(level, coef_ref, perm_ref, panel_ref, part_ref)

    @pl.when(bit_of(0) == 0)
    def _():
        echo_part_ref[...] = mul_t(back_ref[...], pair_weights(panel_ref, last))


def make_plans(perm_ref, slots_refs, chosen_ref, low_ref):
    half = chosen_ref.shape[1]
    for level in range(perm_ref.shape[0]):
        bit = bit_of(level)
        for side in range(2):
            row = half_row(perm_ref, level, bit if side == 0 else 1 - bit)
            if level == 0:
                row = slots_refs[side][...]
            chosen_ref[2 * level + side], low_ref[2 * level + side] = place_plan(row, half)


def bracket_kernel(
    level, coef_ref, perm_ref, map_ref, panel_ref, early_ref, own_slots_ref, out_slots_ref,
    arrived_map_ref, echo_in, leaf_in, slots_in,
    part_ref, kept_map_ref, out_ref, chosen_ref, low_ref, echo_part_ref, back_ref,
    echo, leaf, slots, done,
):
    loads = echo_loads(echo_in, leaf_in, slots_in, echo, leaf, slots, done)
    early = bit_of(0) == 0

    @pl.when(early)
    def _():
        echo_part_ref[...] = early_ref[...]

    @pl.when(jnp.logical_not(early))
    def _():
        for load in loads[:2]:
            load.start()
        make_plans(perm_ref, (own_slots_ref, out_slots_ref), chosen_ref, low_ref)
        echo_back(loads, echo, leaf, slots, back_ref, ((0,), (1,), (2,), (3,)))
        echo_part_ref[...] = mul_t(back_ref[...], pair_weights(panel_ref, level))

    plan = take_plan(half_row(perm_ref, level, bit_of(level)))
    own = take(plan, coef_ref[...]).astype(thin)
    both = mul(twice(own), map_ref[...]) - echo_part_ref[...]
    width = own.shape[1]
    part_ref[...] = both[:, :width]
    out_ref[...] = both[:, width:].astype(thin)
    kept_map_ref[...] = arrived_map_ref[...]


def plan_kernel(
    perm_ref, own_slots_ref, out_slots_ref, chosen_in, low_in, sent_ref, map_ref,
    chosen_ref, low_ref, rest_ref,
):
    del chosen_in, low_in
    rest_ref[...] = mul(sent_ref[...], map_ref[...])

    @pl.when(bit_of(0) == 0)
    def _():
        make_plans(perm_ref, (own_slots_ref, out_slots_ref), chosen_ref, low_ref)


def planned(level, side, chosen_ref, low_ref):
    return chosen_ref[2 * level + side], low_ref[2 * level + side]


def join_kernel(level, arrived_ref, part_ref, map_ref, chosen_ref, low_ref, placed_ref):
    own = part_ref[...] + mul(twice(arrived_ref[...]), map_ref[...])
    plan = planned(level, 0, chosen_ref, low_ref)
    placed_ref[...] = place(plan, own.astype(thin)).astype(thin)


def own_back_kernel(level, coef_ref, panel_ref, chosen_ref, low_ref, placed_ref):
    own = mul_t(coef_ref[...], pair_weight(panel_ref, level, bit_of(level))).astype(thin)
    plan = planned(level, 0, chosen_ref, low_ref)
    placed_ref[...] = place(plan, own).astype(thin)


def backward_kernel(level, arrived_ref, placed_ref, chosen_ref, low_ref, panel_ref, *refs):
    *rest_ref, coef_ref, out_ref = refs
    arrived = arrived_ref[...]
    if rest_ref:
        arrived = (arrived.astype(wide) + rest_ref[0][...]).astype(thin)
    plan = planned(level + 1, 1, chosen_ref, low_ref)
    back = place(plan, arrived) + placed_ref[...].astype(wide)
    back = back.astype(thin)
    coef_ref[...] = back
    weight = pair_weight(panel_ref, level, 1 - bit_of(level))
    out_ref[...] = mul_t(back, weight).astype(thin)


def last_kernel(
    arrived_ref, placed_ref, chosen_ref, low_ref, leaf_ref, scene_ref, image_ref, image, sent
):
    rows = scene_ref.shape[0]
    chunk = rows // scene_chunks
    back = place(planned(0, 1, chosen_ref, low_ref), arrived_ref[...])
    back = unstack((back + placed_ref[...].astype(wide)).astype(thin))
    stores = []
    for at in range(scene_chunks):
        part = pl.ds(at * chunk, chunk)
        gradient = mul_t(back[at * chunk : (at + 1) * chunk], leaf_ref[...])
        image[part] = (scene_ref[part].astype(wide) - step_size * gradient).astype(thin)
        stores.append(pltpu.make_async_copy(image.at[part], image_ref.at[part], sent.at[at]))
        stores[-1].start()
    for store in stores:
        store.wait()


def call(kernel, outs, *operands, far=(), far_out=False, scratch=(), aliases={}):
    shapes = tuple(jax.ShapeDtypeStruct(shape, kind) for shape, kind in outs)
    near, off = pl.BlockSpec(memory_space=pltpu.VMEM), pl.BlockSpec(memory_space=pltpu.HBM)
    away = tuple(pltpu.with_memory_space_constraint(array, pltpu.HBM) for array in far)
    got = pl.pallas_call(
        kernel,
        out_shape=shapes,
        in_specs=[near] * len(operands) + [off] * len(far),
        out_specs=tuple(off if far_out else near for _ in shapes),
        scratch_shapes=scratch,
        input_output_aliases=aliases,
        compiler_params=pltpu.CompilerParams(vmem_limit_bytes=16 * 2**20),
        cost_estimate=pl.CostEstimate(flops=10**6, bytes_accessed=10**4, transcendentals=0),
    )(*operands, *away)
    return got[0] if len(outs) == 1 else got


def like(array):
    return (array.shape, array.dtype)


def on_device(
    scene_image, echoes, pixel_slot, pulse_slot, level_perm, target_leaf, source_leaf, panels
):
    levels = lax.axis_size("box").bit_length() - 1
    rows, samples = scene_image.shape
    half = rows // 2
    width = target_leaf.shape[1]
    column_of = ((half, 2 * width), thin)
    row_half = ((1, half), jnp.int32)
    sent = ((half, width), thin)
    mixed = ((half, 2 * width), wide)

    far = (scene_image, target_leaf, pixel_slot, level_perm, panels)
    scene_near, leaf_near, pixel_near, perms, blocks, leafed, out_slots, outgoing = call(
        first_kernel,
        [like(array) for array in far] + [column_of, row_half, sent],
        far=far,
        scratch=[pltpu.SemaphoreType.DMA((4 + scene_chunks,))],
    )
    arrived = swapped(outgoing, "box", 0)
    place_like = [((half, half), thin), ((half, lanes), thin)]
    own_slots, part = call(
        first_own_kernel, [row_half, mixed], leafed, pixel_near, perms, blocks
    )
    last = levels - 1
    echo_scratch = [
        pltpu.VMEM(echoes.shape, thin),
        pltpu.VMEM(source_leaf.shape, thin),
        pltpu.VMEM(pulse_slot.shape, jnp.int32),
        pltpu.SemaphoreType.DMA((2 + scene_chunks,)),
    ]
    for level in range(1, levels):
        coefficients, outgoing = call(
            functools.partial(forward_kernel, level - 1),
            [column_of, sent],
            arrived,
            part,
            blocks,
            perms,
        )
        arrived = swapped(outgoing, "box", level)
        if level == 1:
            narrow_map = ((2 * width, width), thin)
            part, own_map, other_map, sent_map, early = call(
                functools.partial(own_map_kernel, level, last),
                [mixed, ((2 * width, 2 * width), thin), narrow_map, ((width, width), thin), column_of],
                coefficients,
                perms,
                blocks,
                far=(echoes, source_leaf, pulse_slot),
                scratch=echo_scratch,
            )
            arrived_map = swapped(sent_map, "box", last)
        elif level == 2:
            part, early = call(
                functools.partial(own_echo_kernel, level, last),
                [mixed, mixed],
                coefficients,
                perms,
                blocks,
                early,
            )
        elif level < last:
            part = call(
                functools.partial(own_kernel, level),
                [mixed],
                coefficients,
                perms,
                blocks,
            )
    half_wide = ((half, width), wide)
    plan_like = [((2 * levels, half, half), thin), ((2 * levels, half, lanes), thin)]
    part, arrived_map, bracket, *plans = call(
        functools.partial(bracket_kernel, last),
        [half_wide, ((width, width), thin), sent] + plan_like,
        coefficients,
        perms,
        own_map,
        blocks,
        early,
        own_slots,
        out_slots,
        arrived_map,
        far=(echoes, source_leaf, pulse_slot),
        scratch=[pltpu.VMEM((half, 2 * width), wide), pltpu.VMEM((half, 2 * width), thin)]
        + echo_scratch,
    )
    arrived_bracket = swapped(bracket, "box", last)
    *plans, rest = call(
        plan_kernel,
        plan_like + [half_wide],
        perms,
        own_slots,
        out_slots,
        *plans,
        outgoing,
        arrived_map,
        aliases={3: 0, 4: 1},
    )
    placed = call(
        functools.partial(join_kernel, last), [column_of], arrived, part, other_map, *plans
    )
    arrived, more = arrived_bracket, (rest,)
    for level in reversed(range(last)):
        coefficients, outgoing = call(
            functools.partial(backward_kernel, level),
            [column_of, sent],
            arrived,
            placed,
            *plans,
            blocks,
            *more,
        )
        arrived, more = swapped(outgoing, "box", level), ()
        placed = call(
            functools.partial(own_back_kernel, level), [column_of], coefficients, blocks, *plans
        )
    return call(
        last_kernel,
        [((rows, samples), thin)],
        arrived,
        placed,
        *plans,
        leaf_near,
        scene_near,
        far_out=True,
        scratch=[
            pltpu.VMEM((rows, samples), thin),
            pltpu.SemaphoreType.DMA((scene_chunks,)),
        ],
    )


def solution(mesh):
    return jax.shard_map(
        on_device,
        mesh=mesh,
        in_specs=(
            P(("groups", "box"), None),
            P(("groups", "box"), None),
            P(("groups", "box"), None),
            P(("groups", "box"), None),
            P(None, "box", None),
            P(),
            P(),
            P(None, "box", None, None, None),
        ),
        out_specs=P(("groups", "box"), None),
        check_vma=False,
    )
```

```python
import functools

import jax
import jax.numpy as jnp
from jax import lax
from jax.experimental import pallas as pl
from jax.experimental.pallas import tpu as pltpu
from jax.sharding import PartitionSpec as P

step_size = 0.1
wide = jnp.float32
thin = jnp.bfloat16
lanes = 128
scene_chunks = 4


def swapped(value, axis, apart):
    return lax.ppermute(value, axis, [(i, i ^ 1 << apart) for i in range(lax.axis_size(axis))])


def mul(left, right):
    return jnp.dot(left, right, preferred_element_type=wide)


def mul_t(left, right):
    return lax.dot_general(left, right, (((1,), (1,)), ((), ())), preferred_element_type=wide)


def bit_of(level):
    return lax.axis_index("box") // 2**level % 2


def half_row(perm_ref, level, which):
    half = perm_ref.shape[2] // 2
    return perm_ref[level, :, pl.ds(pl.multiple_of(which * half, half), half)]


def column(row):
    parts = []
    for at in range(0, row.shape[1], lanes):
        parts.append(jnp.broadcast_to(row[:, at : at + lanes], (lanes, lanes)).T)
    return jnp.concatenate(parts, axis=0)


def one_hot(hits):
    return jnp.where(hits, 1.0, 0.0).astype(thin)


def fold(slots, half):
    return jnp.where(slots < half, slots, slots - half)


def take_plan(row):
    half = row.shape[1]
    slots = column(row)
    within = fold(slots, half)
    lane = lax.broadcasted_iota(jnp.int32, slots.shape, 1)
    chosen = [one_hot(within == lane + at) for at in range(0, half, lanes)]
    return jnp.concatenate(chosen, axis=1), jnp.where(slots < half, 1.0, 0.0)


def take(plan, both):
    chosen, low = plan
    total = mul(chosen, both)
    width = both.shape[1] // 2
    return jnp.where(low > 0.5, total[:, :width], total[:, width:])


def place_plan(row, half):
    target = lax.broadcasted_iota(jnp.int32, (half, row.shape[1]), 0)
    return one_hot(target == fold(row, half)), one_hot(column(row) < half)


def place(plan, values):
    chosen, low = plan
    return mul(chosen, jnp.concatenate([values * low, values * (1 - low)], axis=1))


def compose(outer, inner):
    half = outer.shape[1] // 2
    digits = jnp.concatenate([outer // 256, outer % 256], axis=0).astype(wide)
    digits = jnp.concatenate([digits[:, :half], digits[:, half:]], axis=0)
    digits = jnp.pad(digits, ((0, 12), (0, 0))).astype(thin)
    target = lax.broadcasted_iota(jnp.int32, (half, inner.shape[1]), 0)
    total = mul(digits, one_hot(target == fold(inner, half)))
    picked = jnp.where(inner < half, total[0:2], total[2:4])
    return (picked[0:1] * 256 + picked[1:2]).astype(jnp.int32)


def stack(values):
    half = values.shape[0] // 2
    return jnp.concatenate([values[:half], values[half:]], axis=1)


def unstack(values):
    width = values.shape[1] // 2
    return jnp.concatenate([values[:, :width], values[:, width:]], axis=0)


def pair_weight(panel_ref, level, which):
    return jnp.concatenate(
        [panel_ref[level, 0, which], panel_ref[level, 0, 2 + which]], axis=1
    )


def pair_weights(panel_ref, level):
    bit = bit_of(level)
    own, other = pair_weight(panel_ref, level, bit), pair_weight(panel_ref, level, 1 - bit)
    return jnp.concatenate([own, other], axis=0)


def first_kernel(
    scene_in, leaf_in, pixel_in, perm_in, panel_in,
    scene_ref, leaf_ref, pixel_ref, perm_ref, panel_ref, leafed_ref, slots_ref, out_ref, done,
):
    rows = scene_ref.shape[0]
    half, width = rows // 2, leaf_ref.shape[1]
    chunk = rows // scene_chunks
    parts = [pl.ds(at * chunk, chunk) for at in range(scene_chunks)]
    pairs = [(pixel_in, pixel_ref), (perm_in, perm_ref), (leaf_in, leaf_ref)]
    pairs += [(scene_in.at[part], scene_ref.at[part]) for part in parts]
    pairs += [(panel_in, panel_ref)]
    loads = [
        pltpu.make_async_copy(source, target, done.at[at])
        for at, (source, target) in enumerate(pairs)
    ]
    for at in (0, 1, 2, 3, 5, 4, 6, 7):
        loads[at].start()
    loads[0].wait()
    loads[1].wait()
    slots = compose(pixel_ref[...], half_row(perm_ref, 0, 1 - bit_of(0)))
    slots_ref[...] = slots
    chosen, low = take_plan(slots)
    loads[2].wait()
    total = None
    for at in range(0, half, chunk):
        loads[3 + at // chunk].wait()
        loads[3 + (half + at) // chunk].wait()
        pieces = [
            mul(scene_ref[pl.ds(side * half + at, chunk)], leaf_ref[...]).astype(thin)
            for side in range(2)
        ]
        both = jnp.concatenate(pieces, axis=1)
        leafed_ref[pl.ds(at, chunk)] = both
        piece = mul(chosen[:, at : at + chunk], both)
        total = piece if total is None else total + piece
    out_ref[...] = jnp.where(low > 0.5, total[:, :width], total[:, width:]).astype(thin)
    loads[-1].wait()


def first_own_kernel(leafed_ref, pixel_ref, perm_ref, panel_ref, slots_ref, part_ref):
    bit = bit_of(0)
    slots = compose(pixel_ref[...], half_row(perm_ref, 0, bit))
    slots_ref[...] = slots
    own = take(take_plan(slots), leafed_ref[...]).astype(thin)
    part_ref[...] = mul(own, pair_weight(panel_ref, 0, bit))


def own_kernel(level, coef_ref, perm_ref, panel_ref, part_ref):
    bit = bit_of(level)
    own = take(take_plan(half_row(perm_ref, level, bit)), coef_ref[...]).astype(thin)
    part_ref[...] = mul(own, pair_weight(panel_ref, level, bit))


def split(values):
    high = values.astype(thin)
    return jnp.concatenate([high, (values - high.astype(wide)).astype(thin)], axis=0)


def twice(values):
    return jnp.concatenate([values, values], axis=1)


def echo_loads(echo_in, leaf_in, slots_in, echo, leaf, slots, done):
    rows = echo.shape[0]
    chunk = rows // scene_chunks
    parts = [pl.ds(at * chunk, chunk) for at in range(scene_chunks)]
    pairs = [(slots_in, slots), (leaf_in, leaf)]
    pairs += [(echo_in.at[part], echo.at[part]) for part in parts]
    return [
        pltpu.make_async_copy(source, target, done.at[at])
        for at, (source, target) in enumerate(pairs)
    ]


def echo_back(loads, echo, leaf, slots, back_ref, turns):
    half = echo.shape[0] // 2
    chunk = echo.shape[0] // scene_chunks
    for at in turns[0] if turns else ():
        loads[2 + at].start()
    loads[0].wait()
    plan = place_plan(slots[...], half)
    if turns:
        loads[1].wait()
    else:
        for load in loads[2:]:
            load.wait()
    back = []
    for turn in turns or (range(scene_chunks),):
        for at in turn if turns and turn != turns[0] else ():
            loads[2 + at].start()
        for at in turn:
            if turns:
                loads[2 + at].wait()
            back.append(mul_t(echo[pl.ds(at * chunk, chunk)], leaf[...]).astype(thin))
    back_ref[...] = place(plan, jnp.concatenate(back, axis=0)).astype(thin)


def own_map_kernel(
    level, last, coef_ref, perm_ref, panel_ref, echo_in, leaf_in, slots_in,
    part_ref, own_map_ref, other_map_ref, sent_map_ref, echo_part_ref, back_ref,
    echo, leaf, slots, done,
):
    loads = echo_loads(echo_in, leaf_in, slots_in, echo, leaf, slots, done)
    early = bit_of(0) == 0

    @pl.when(early)
    def _():
        for load in loads:
            load.start()

    @pl.when(jnp.logical_not(early))
    def _():
        loads[1].start()

    own_kernel(level, coef_ref, perm_ref, panel_ref, part_ref)
    loads[1].wait()
    gram = split(mul_t(leaf[...], leaf[...]))
    both = pair_weights(panel_ref, last)
    width = both.shape[0] // 2
    scaled = stack(mul(twice(unstack(both)), gram))
    pair = mul_t(split(scaled), both)
    maps = pair[: 2 * width] + pair[2 * width :]
    own_map_ref[...] = split(maps[:width])
    other_map_ref[...] = split(maps[width:, :width])
    sent_map_ref[...] = maps[width:, width:].astype(thin)

    @pl.when(early)
    def _():
        echo_back(loads, echo, leaf, slots, back_ref, None)
        echo_part_ref[...] = mul_t(back_ref[...], both)


def mix(level, arrived_ref, part_ref, panel_ref):
    weight = pair_weight(panel_ref, level, 1 - bit_of(level))
    mixture = part_ref[...] + mul(arrived_ref[...], weight)
    return mixture.astype(thin)


def forward_kernel(level, arrived_ref, part_ref, panel_ref, perm_ref, coef_ref, out_ref):
    weight = pair_weight(panel_ref, level, 1 - bit_of(level))
    chosen, low = take_plan(half_row(perm_ref, level + 1, 1 - bit_of(level + 1)))
    half, width = arrived_ref.shape
    step = half // 2
    total = None
    for at in range(0, half, step):
        part = pl.ds(at, step)
        mixture = (part_ref[part] + mul(arrived_ref[part], weight)).astype(thin)
        coef_ref[part] = mixture
        piece = mul(chosen[:, at : at + step], mixture)
        total = piece if total is None else total + piece
    out_ref[...] = jnp.where(low > 0.5, total[:, :width], total[:, width:]).astype(thin)


def make_plans(perm_ref, slots_refs, chosen_ref, low_ref):
    half = chosen_ref.shape[1]
    for level in range(perm_ref.shape[0]):
        bit = bit_of(level)
        for side in range(2):
            row = half_row(perm_ref, level, bit if side == 0 else 1 - bit)
            if level == 0:
                row = slots_refs[side][...]
            chosen_ref[2 * level + side], low_ref[2 * level + side] = place_plan(row, half)


def bracket_kernel(
    level, coef_ref, perm_ref, map_ref, panel_ref, early_ref, own_slots_ref, out_slots_ref,
    arrived_map_ref, echo_in, leaf_in, slots_in,
    part_ref, kept_map_ref, out_ref, chosen_ref, low_ref, echo_part_ref, back_ref,
    echo, leaf, slots, done,
):
    loads = echo_loads(echo_in, leaf_in, slots_in, echo, leaf, slots, done)
    early = bit_of(0) == 0

    @pl.when(early)
    def _():
        echo_part_ref[...] = early_ref[...]

    @pl.when(jnp.logical_not(early))
    def _():
        for load in loads[:2]:
            load.start()
        make_plans(perm_ref, (own_slots_ref, out_slots_ref), chosen_ref, low_ref)
        echo_back(loads, echo, leaf, slots, back_ref, ((0,), (1,), (2,), (3,)))
        echo_part_ref[...] = mul_t(back_ref[...], pair_weights(panel_ref, level))

    plan = take_plan(half_row(perm_ref, level, bit_of(level)))
    own = take(plan, coef_ref[...]).astype(thin)
    both = mul(twice(own), map_ref[...]) - echo_part_ref[...]
    width = own.shape[1]
    part_ref[...] = both[:, :width]
    out_ref[...] = both[:, width:].astype(thin)
    kept_map_ref[...] = arrived_map_ref[...]


def plan_kernel(
    perm_ref, own_slots_ref, out_slots_ref, chosen_in, low_in, sent_ref, map_ref,
    chosen_ref, low_ref, rest_ref,
):
    del chosen_in, low_in
    rest_ref[...] = mul(sent_ref[...], map_ref[...])

    @pl.when(bit_of(0) == 0)
    def _():
        make_plans(perm_ref, (own_slots_ref, out_slots_ref), chosen_ref, low_ref)


def planned(level, side, chosen_ref, low_ref):
    return chosen_ref[2 * level + side], low_ref[2 * level + side]


def join_kernel(level, arrived_ref, part_ref, map_ref, chosen_ref, low_ref, placed_ref):
    own = part_ref[...] + mul(twice(arrived_ref[...]), map_ref[...])
    plan = planned(level, 0, chosen_ref, low_ref)
    placed_ref[...] = place(plan, own.astype(thin)).astype(thin)


def own_back_kernel(level, coef_ref, panel_ref, chosen_ref, low_ref, placed_ref):
    own = mul_t(coef_ref[...], pair_weight(panel_ref, level, bit_of(level))).astype(thin)
    plan = planned(level, 0, chosen_ref, low_ref)
    placed_ref[...] = place(plan, own).astype(thin)


def backward_kernel(level, arrived_ref, placed_ref, chosen_ref, low_ref, panel_ref, *refs):
    *rest_ref, coef_ref, out_ref = refs
    arrived = arrived_ref[...]
    if rest_ref:
        arrived = (arrived.astype(wide) + rest_ref[0][...]).astype(thin)
    plan = planned(level + 1, 1, chosen_ref, low_ref)
    back = place(plan, arrived) + placed_ref[...].astype(wide)
    back = back.astype(thin)
    coef_ref[...] = back
    weight = pair_weight(panel_ref, level, 1 - bit_of(level))
    out_ref[...] = mul_t(back, weight).astype(thin)


def last_kernel(
    arrived_ref, placed_ref, chosen_ref, low_ref, leaf_ref, scene_ref, image_ref, image, sent
):
    rows = scene_ref.shape[0]
    chunk = rows // scene_chunks
    back = place(planned(0, 1, chosen_ref, low_ref), arrived_ref[...])
    back = unstack((back + placed_ref[...].astype(wide)).astype(thin))
    stores = []
    for at in range(scene_chunks):
        part = pl.ds(at * chunk, chunk)
        gradient = mul_t(back[at * chunk : (at + 1) * chunk], leaf_ref[...])
        image[part] = (scene_ref[part].astype(wide) - step_size * gradient).astype(thin)
        stores.append(pltpu.make_async_copy(image.at[part], image_ref.at[part], sent.at[at]))
        stores[-1].start()
    for store in stores:
        store.wait()


def call(kernel, outs, *operands, far=(), far_out=False, scratch=(), aliases={}):
    shapes = tuple(jax.ShapeDtypeStruct(shape, kind) for shape, kind in outs)
    near, off = pl.BlockSpec(memory_space=pltpu.VMEM), pl.BlockSpec(memory_space=pltpu.HBM)
    away = tuple(pltpu.with_memory_space_constraint(array, pltpu.HBM) for array in far)
    got = pl.pallas_call(
        kernel,
        out_shape=shapes,
        in_specs=[near] * len(operands) + [off] * len(far),
        out_specs=tuple(off if far_out else near for _ in shapes),
        scratch_shapes=scratch,
        input_output_aliases=aliases,
        compiler_params=pltpu.CompilerParams(vmem_limit_bytes=16 * 2**20),
        cost_estimate=pl.CostEstimate(flops=10**6, bytes_accessed=10**4, transcendentals=0),
    )(*operands, *away)
    return got[0] if len(outs) == 1 else got


def like(array):
    return (array.shape, array.dtype)


def on_device(
    scene_image, echoes, pixel_slot, pulse_slot, level_perm, target_leaf, source_leaf, panels
):
    levels = lax.axis_size("box").bit_length() - 1
    rows, samples = scene_image.shape
    half = rows // 2
    width = target_leaf.shape[1]
    column_of = ((half, 2 * width), thin)
    row_half = ((1, half), jnp.int32)
    sent = ((half, width), thin)
    mixed = ((half, 2 * width), wide)

    far = (scene_image, target_leaf, pixel_slot, level_perm, panels)
    scene_near, leaf_near, pixel_near, perms, blocks, leafed, out_slots, outgoing = call(
        first_kernel,
        [like(array) for array in far] + [column_of, row_half, sent],
        far=far,
        scratch=[pltpu.SemaphoreType.DMA((4 + scene_chunks,))],
    )
    arrived = swapped(outgoing, "box", 0)
    place_like = [((half, half), thin), ((half, lanes), thin)]
    own_slots, part = call(
        first_own_kernel, [row_half, mixed], leafed, pixel_near, perms, blocks
    )
    last = levels - 1
    echo_scratch = [
        pltpu.VMEM(echoes.shape, thin),
        pltpu.VMEM(source_leaf.shape, thin),
        pltpu.VMEM(pulse_slot.shape, jnp.int32),
        pltpu.SemaphoreType.DMA((2 + scene_chunks,)),
    ]
    for level in range(1, levels):
        coefficients, outgoing = call(
            functools.partial(forward_kernel, level - 1),
            [column_of, sent],
            arrived,
            part,
            blocks,
            perms,
        )
        arrived = swapped(outgoing, "box", level)
        if level == 1:
            narrow_map = ((2 * width, width), thin)
            part, own_map, other_map, sent_map, early = call(
                functools.partial(own_map_kernel, level, last),
                [mixed, ((2 * width, 2 * width), thin), narrow_map, ((width, width), thin), mixed],
                coefficients,
                perms,
                blocks,
                far=(echoes, source_leaf, pulse_slot),
                scratch=[pltpu.VMEM((half, 2 * width), thin)] + echo_scratch,
            )
            arrived_map = swapped(sent_map, "box", last)
        elif level < last:
            part = call(
                functools.partial(own_kernel, level),
                [mixed],
                coefficients,
                perms,
                blocks,
            )
    half_wide = ((half, width), wide)
    plan_like = [((2 * levels, half, half), thin), ((2 * levels, half, lanes), thin)]
    part, arrived_map, bracket, *plans = call(
        functools.partial(bracket_kernel, last),
        [half_wide, ((width, width), thin), sent] + plan_like,
        coefficients,
        perms,
        own_map,
        blocks,
        early,
        own_slots,
        out_slots,
        arrived_map,
        far=(echoes, source_leaf, pulse_slot),
        scratch=[pltpu.VMEM((half, 2 * width), wide), pltpu.VMEM((half, 2 * width), thin)]
        + echo_scratch,
    )
    arrived_bracket = swapped(bracket, "box", last)
    *plans, rest = call(
        plan_kernel,
        plan_like + [half_wide],
        perms,
        own_slots,
        out_slots,
        *plans,
        outgoing,
        arrived_map,
        aliases={3: 0, 4: 1},
    )
    placed = call(
        functools.partial(join_kernel, last), [column_of], arrived, part, other_map, *plans
    )
    arrived, more = arrived_bracket, (rest,)
    for level in reversed(range(last)):
        coefficients, outgoing = call(
            functools.partial(backward_kernel, level),
            [column_of, sent],
            arrived,
            placed,
            *plans,
            blocks,
            *more,
        )
        arrived, more = swapped(outgoing, "box", level), ()
        placed = call(
            functools.partial(own_back_kernel, level), [column_of], coefficients, blocks, *plans
        )
    return call(
        last_kernel,
        [((rows, samples), thin)],
        arrived,
        placed,
        *plans,
        leaf_near,
        scene_near,
        far_out=True,
        scratch=[
            pltpu.VMEM((rows, samples), thin),
            pltpu.SemaphoreType.DMA((scene_chunks,)),
        ],
    )


def solution(mesh):
    return jax.shard_map(
        on_device,
        mesh=mesh,
        in_specs=(
            P(("groups", "box"), None),
            P(("groups", "box"), None),
            P(("groups", "box"), None),
            P(("groups", "box"), None),
            P(None, "box", None),
            P(),
            P(),
            P(None, "box", None, None, None),
        ),
        out_specs=P(("groups", "box"), None),
        check_vma=False,
    )
```

```python
import functools

import jax
import jax.numpy as jnp
from jax import lax
from jax.experimental import pallas as pl
from jax.experimental.pallas import tpu as pltpu
from jax.sharding import PartitionSpec as P

step_size = 0.1
wide = jnp.float32
thin = jnp.bfloat16
lanes = 128
scene_chunks = 4


def swapped(value, axis, apart):
    return lax.ppermute(value, axis, [(i, i ^ 1 << apart) for i in range(lax.axis_size(axis))])


def mul(left, right):
    return jnp.dot(left, right, preferred_element_type=wide)


def mul_t(left, right):
    return lax.dot_general(left, right, (((1,), (1,)), ((), ())), preferred_element_type=wide)


def bit_of(level):
    return lax.axis_index("box") // 2**level % 2


def half_row(perm_ref, level, which):
    half = perm_ref.shape[2] // 2
    return perm_ref[level, :, pl.ds(pl.multiple_of(which * half, half), half)]


def column(row):
    parts = []
    for at in range(0, row.shape[1], lanes):
        parts.append(jnp.broadcast_to(row[:, at : at + lanes], (lanes, lanes)).T)
    return jnp.concatenate(parts, axis=0)


def one_hot(hits):
    return jnp.where(hits, 1.0, 0.0).astype(thin)


def fold(slots, half):
    return jnp.where(slots < half, slots, slots - half)


def take_plan(row):
    half = row.shape[1]
    slots = column(row)
    within = fold(slots, half)
    lane = lax.broadcasted_iota(jnp.int32, slots.shape, 1)
    chosen = [one_hot(within == lane + at) for at in range(0, half, lanes)]
    return jnp.concatenate(chosen, axis=1), jnp.where(slots < half, 1.0, 0.0)


def take(plan, both):
    chosen, low = plan
    total = mul(chosen, both)
    width = both.shape[1] // 2
    return jnp.where(low > 0.5, total[:, :width], total[:, width:])


def place_plan(row, half):
    target = lax.broadcasted_iota(jnp.int32, (half, row.shape[1]), 0)
    return one_hot(target == fold(row, half)), one_hot(column(row) < half)


def place(plan, values):
    chosen, low = plan
    return mul(chosen, jnp.concatenate([values * low, values * (1 - low)], axis=1))


def compose(outer, inner):
    half = outer.shape[1] // 2
    digits = jnp.concatenate([outer // 256, outer % 256], axis=0).astype(wide)
    digits = jnp.concatenate([digits[:, :half], digits[:, half:]], axis=0)
    digits = jnp.pad(digits, ((0, 12), (0, 0))).astype(thin)
    target = lax.broadcasted_iota(jnp.int32, (half, inner.shape[1]), 0)
    total = mul(digits, one_hot(target == fold(inner, half)))
    picked = jnp.where(inner < half, total[0:2], total[2:4])
    return (picked[0:1] * 256 + picked[1:2]).astype(jnp.int32)


def stack(values):
    half = values.shape[0] // 2
    return jnp.concatenate([values[:half], values[half:]], axis=1)


def unstack(values):
    width = values.shape[1] // 2
    return jnp.concatenate([values[:, :width], values[:, width:]], axis=0)


def pair_weight(panel_ref, level, which):
    return jnp.concatenate(
        [panel_ref[level, 0, which], panel_ref[level, 0, 2 + which]], axis=1
    )


def pair_weights(panel_ref, level):
    bit = bit_of(level)
    own, other = pair_weight(panel_ref, level, bit), pair_weight(panel_ref, level, 1 - bit)
    return jnp.concatenate([own, other], axis=0)


def first_kernel(
    scene_in, leaf_in, pixel_in, perm_in, panel_in,
    scene_ref, leaf_ref, pixel_ref, perm_ref, panel_ref, leafed_ref, slots_ref, out_ref, done,
):
    rows = scene_ref.shape[0]
    half, width = rows // 2, leaf_ref.shape[1]
    chunk = rows // scene_chunks
    parts = [pl.ds(at * chunk, chunk) for at in range(scene_chunks)]
    pairs = [(pixel_in, pixel_ref), (perm_in, perm_ref), (leaf_in, leaf_ref)]
    pairs += [(scene_in.at[part], scene_ref.at[part]) for part in parts]
    pairs += [(panel_in, panel_ref)]
    loads = [
        pltpu.make_async_copy(source, target, done.at[at])
        for at, (source, target) in enumerate(pairs)
    ]
    for at in (0, 1, 2, 3, 5, 4, 6, 7):
        loads[at].start()
    loads[0].wait()
    loads[1].wait()
    slots = compose(pixel_ref[...], half_row(perm_ref, 0, 1 - bit_of(0)))
    slots_ref[...] = slots
    chosen, low = take_plan(slots)
    loads[2].wait()
    total = None
    for at in range(0, half, chunk):
        loads[3 + at // chunk].wait()
        loads[3 + (half + at) // chunk].wait()
        pieces = [
            mul(scene_ref[pl.ds(side * half + at, chunk)], leaf_ref[...]).astype(thin)
            for side in range(2)
        ]
        both = jnp.concatenate(pieces, axis=1)
        leafed_ref[pl.ds(at, chunk)] = both
        piece = mul(chosen[:, at : at + chunk], both)
        total = piece if total is None else total + piece
    out_ref[...] = jnp.where(low > 0.5, total[:, :width], total[:, width:]).astype(thin)
    loads[-1].wait()


def first_own_kernel(leafed_ref, pixel_ref, perm_ref, panel_ref, slots_ref, part_ref):
    bit = bit_of(0)
    slots = compose(pixel_ref[...], half_row(perm_ref, 0, bit))
    slots_ref[...] = slots
    own = take(take_plan(slots), leafed_ref[...]).astype(thin)
    part_ref[...] = mul(own, pair_weight(panel_ref, 0, bit))


def own_kernel(level, coef_ref, perm_ref, panel_ref, part_ref):
    bit = bit_of(level)
    own = take(take_plan(half_row(perm_ref, level, bit)), coef_ref[...]).astype(thin)
    part_ref[...] = mul(own, pair_weight(panel_ref, level, bit))


def split(values):
    high = values.astype(thin)
    return jnp.concatenate([high, (values - high.astype(wide)).astype(thin)], axis=0)


def twice(values):
    return jnp.concatenate([values, values], axis=1)


def echo_loads(echo_in, leaf_in, slots_in, echo, leaf, slots, done):
    rows = echo.shape[0]
    chunk = rows // scene_chunks
    parts = [pl.ds(at * chunk, chunk) for at in range(scene_chunks)]
    pairs = [(slots_in, slots), (leaf_in, leaf)]
    pairs += [(echo_in.at[part], echo.at[part]) for part in parts]
    return [
        pltpu.make_async_copy(source, target, done.at[at])
        for at, (source, target) in enumerate(pairs)
    ]


def echo_back(loads, echo, leaf, slots, back_ref, turns):
    half = echo.shape[0] // 2
    chunk = echo.shape[0] // scene_chunks
    for at in turns[0] if turns else ():
        loads[2 + at].start()
    loads[0].wait()
    plan = place_plan(slots[...], half)
    if turns:
        loads[1].wait()
    else:
        for load in loads[2:]:
            load.wait()
    back = []
    for turn in turns or (range(scene_chunks),):
        for at in turn if turns and turn != turns[0] else ():
            loads[2 + at].start()
        for at in turn:
            if turns:
                loads[2 + at].wait()
            back.append(mul_t(echo[pl.ds(at * chunk, chunk)], leaf[...]).astype(thin))
    back_ref[...] = place(plan, jnp.concatenate(back, axis=0)).astype(thin)


def own_map_kernel(
    level, last, coef_ref, perm_ref, panel_ref, echo_in, leaf_in, slots_in,
    part_ref, own_map_ref, other_map_ref, sent_map_ref, back_ref, echo, leaf, slots, done,
):
    loads = echo_loads(echo_in, leaf_in, slots_in, echo, leaf, slots, done)
    early = bit_of(0) == 0

    @pl.when(early)
    def _():
        for load in loads:
            load.start()

    @pl.when(jnp.logical_not(early))
    def _():
        loads[1].start()

    own_kernel(level, coef_ref, perm_ref, panel_ref, part_ref)
    loads[1].wait()
    gram = split(mul_t(leaf[...], leaf[...]))
    both = pair_weights(panel_ref, last)
    width = both.shape[0] // 2
    scaled = stack(mul(twice(unstack(both)), gram))
    pair = mul_t(split(scaled), both)
    maps = pair[: 2 * width] + pair[2 * width :]
    own_map_ref[...] = split(maps[:width])
    other_map_ref[...] = split(maps[width:, :width])
    sent_map_ref[...] = maps[width:, width:].astype(thin)

    @pl.when(early)
    def _():
        echo_back(loads, echo, leaf, slots, back_ref, None)


def mix(level, arrived_ref, part_ref, panel_ref):
    weight = pair_weight(panel_ref, level, 1 - bit_of(level))
    mixture = part_ref[...] + mul(arrived_ref[...], weight)
    return mixture.astype(thin)


def forward_kernel(level, arrived_ref, part_ref, panel_ref, perm_ref, coef_ref, out_ref):
    weight = pair_weight(panel_ref, level, 1 - bit_of(level))
    chosen, low = take_plan(half_row(perm_ref, level + 1, 1 - bit_of(level + 1)))
    half, width = arrived_ref.shape
    step = half // 2
    total = None
    for at in range(0, half, step):
        part = pl.ds(at, step)
        mixture = (part_ref[part] + mul(arrived_ref[part], weight)).astype(thin)
        coef_ref[part] = mixture
        piece = mul(chosen[:, at : at + step], mixture)
        total = piece if total is None else total + piece
    out_ref[...] = jnp.where(low > 0.5, total[:, :width], total[:, width:]).astype(thin)


def own_echo_kernel(
    level, last, coef_ref, perm_ref, panel_ref, back_ref, part_ref, echo_part_ref
):
    own_kernel(level, coef_ref, perm_ref, panel_ref, part_ref)

    @pl.when(bit_of(0) == 0)
    def _():
        echo_part_ref[...] = mul_t(back_ref[...], pair_weights(panel_ref, last))


def make_plans(perm_ref, slots_refs, chosen_ref, low_ref):
    half = chosen_ref.shape[1]
    for level in range(perm_ref.shape[0]):
        bit = bit_of(level)
        for side in range(2):
            row = half_row(perm_ref, level, bit if side == 0 else 1 - bit)
            if level == 0:
                row = slots_refs[side][...]
            chosen_ref[2 * level + side], low_ref[2 * level + side] = place_plan(row, half)


def bracket_kernel(
    level, coef_ref, perm_ref, map_ref, panel_ref, early_ref, own_slots_ref, out_slots_ref,
    arrived_map_ref, echo_in, leaf_in, slots_in,
    part_ref, kept_map_ref, out_ref, chosen_ref, low_ref, echo_part_ref, back_ref,
    echo, leaf, slots, done,
):
    loads = echo_loads(echo_in, leaf_in, slots_in, echo, leaf, slots, done)
    early = bit_of(0) == 0

    @pl.when(early)
    def _():
        echo_part_ref[...] = early_ref[...]

    @pl.when(jnp.logical_not(early))
    def _():
        for load in loads[:2]:
            load.start()
        make_plans(perm_ref, (own_slots_ref, out_slots_ref), chosen_ref, low_ref)
        echo_back(loads, echo, leaf, slots, back_ref, ((0,), (1,), (2,), (3,)))
        echo_part_ref[...] = mul_t(back_ref[...], pair_weights(panel_ref, level))

    plan = take_plan(half_row(perm_ref, level, bit_of(level)))
    own = take(plan, coef_ref[...]).astype(thin)
    both = mul(twice(own), map_ref[...]) - echo_part_ref[...]
    width = own.shape[1]
    part_ref[...] = both[:, :width]
    out_ref[...] = both[:, width:].astype(thin)
    kept_map_ref[...] = arrived_map_ref[...]


def plan_kernel(
    perm_ref, own_slots_ref, out_slots_ref, chosen_in, low_in, sent_ref, map_ref,
    chosen_ref, low_ref, rest_ref,
):
    del chosen_in, low_in
    rest_ref[...] = mul(sent_ref[...], map_ref[...])

    @pl.when(bit_of(0) == 0)
    def _():
        make_plans(perm_ref, (own_slots_ref, out_slots_ref), chosen_ref, low_ref)


def planned(level, side, chosen_ref, low_ref):
    return chosen_ref[2 * level + side], low_ref[2 * level + side]


def join_kernel(level, arrived_ref, part_ref, map_ref, chosen_ref, low_ref, placed_ref):
    own = part_ref[...] + mul(twice(arrived_ref[...]), map_ref[...])
    plan = planned(level, 0, chosen_ref, low_ref)
    placed_ref[...] = place(plan, own.astype(thin)).astype(thin)


def own_back_kernel(level, coef_ref, panel_ref, chosen_ref, low_ref, placed_ref):
    own = mul_t(coef_ref[...], pair_weight(panel_ref, level, bit_of(level))).astype(thin)
    plan = planned(level, 0, chosen_ref, low_ref)
    placed_ref[...] = place(plan, own).astype(thin)


def backward_kernel(level, arrived_ref, placed_ref, chosen_ref, low_ref, panel_ref, *refs):
    *rest_ref, coef_ref, out_ref = refs
    arrived = arrived_ref[...]
    if rest_ref:
        arrived = (arrived.astype(wide) + rest_ref[0][...]).astype(thin)
    plan = planned(level + 1, 1, chosen_ref, low_ref)
    back = place(plan, arrived) + placed_ref[...].astype(wide)
    back = back.astype(thin)
    coef_ref[...] = back
    weight = pair_weight(panel_ref, level, 1 - bit_of(level))
    out_ref[...] = mul_t(back, weight).astype(thin)


def last_kernel(
    arrived_ref, placed_ref, chosen_ref, low_ref, leaf_ref, scene_ref, image_ref, image, sent
):
    rows = scene_ref.shape[0]
    chunk = rows // scene_chunks
    back = place(planned(0, 1, chosen_ref, low_ref), arrived_ref[...])
    back = unstack((back + placed_ref[...].astype(wide)).astype(thin))
    stores = []
    for at in range(scene_chunks):
        part = pl.ds(at * chunk, chunk)
        gradient = mul_t(back[at * chunk : (at + 1) * chunk], leaf_ref[...])
        image[part] = (scene_ref[part].astype(wide) - step_size * gradient).astype(thin)
        stores.append(pltpu.make_async_copy(image.at[part], image_ref.at[part], sent.at[at]))
        stores[-1].start()
    for store in stores:
        store.wait()


def call(kernel, outs, *operands, far=(), far_out=False, scratch=(), aliases={}):
    shapes = tuple(jax.ShapeDtypeStruct(shape, kind) for shape, kind in outs)
    near, off = pl.BlockSpec(memory_space=pltpu.VMEM), pl.BlockSpec(memory_space=pltpu.HBM)
    away = tuple(pltpu.with_memory_space_constraint(array, pltpu.HBM) for array in far)
    got = pl.pallas_call(
        kernel,
        out_shape=shapes,
        in_specs=[near] * len(operands) + [off] * len(far),
        out_specs=tuple(off if far_out else near for _ in shapes),
        scratch_shapes=scratch,
        input_output_aliases=aliases,
        compiler_params=pltpu.CompilerParams(vmem_limit_bytes=16 * 2**20),
        cost_estimate=pl.CostEstimate(flops=10**6, bytes_accessed=10**4, transcendentals=0),
    )(*operands, *away)
    return got[0] if len(outs) == 1 else got


def like(array):
    return (array.shape, array.dtype)


def on_device(
    scene_image, echoes, pixel_slot, pulse_slot, level_perm, target_leaf, source_leaf, panels
):
    levels = lax.axis_size("box").bit_length() - 1
    rows, samples = scene_image.shape
    half = rows // 2
    width = target_leaf.shape[1]
    column_of = ((half, 2 * width), thin)
    row_half = ((1, half), jnp.int32)
    sent = ((half, width), thin)
    mixed = ((half, 2 * width), wide)

    far = (scene_image, target_leaf, pixel_slot, level_perm, panels)
    scene_near, leaf_near, pixel_near, perms, blocks, leafed, out_slots, outgoing = call(
        first_kernel,
        [like(array) for array in far] + [column_of, row_half, sent],
        far=far,
        scratch=[pltpu.SemaphoreType.DMA((4 + scene_chunks,))],
    )
    arrived = swapped(outgoing, "box", 0)
    place_like = [((half, half), thin), ((half, lanes), thin)]
    own_slots, part = call(
        first_own_kernel, [row_half, mixed], leafed, pixel_near, perms, blocks
    )
    last = levels - 1
    echo_scratch = [
        pltpu.VMEM(echoes.shape, thin),
        pltpu.VMEM(source_leaf.shape, thin),
        pltpu.VMEM(pulse_slot.shape, jnp.int32),
        pltpu.SemaphoreType.DMA((2 + scene_chunks,)),
    ]
    for level in range(1, levels):
        coefficients, outgoing = call(
            functools.partial(forward_kernel, level - 1),
            [column_of, sent],
            arrived,
            part,
            blocks,
            perms,
        )
        arrived = swapped(outgoing, "box", level)
        if level == 1:
            narrow_map = ((2 * width, width), thin)
            part, own_map, other_map, sent_map, early = call(
                functools.partial(own_map_kernel, level, last),
                [mixed, ((2 * width, 2 * width), thin), narrow_map, ((width, width), thin), column_of],
                coefficients,
                perms,
                blocks,
                far=(echoes, source_leaf, pulse_slot),
                scratch=echo_scratch,
            )
            arrived_map = swapped(sent_map, "box", last)
        elif level == 2:
            part, early = call(
                functools.partial(own_echo_kernel, level, last),
                [mixed, mixed],
                coefficients,
                perms,
                blocks,
                early,
            )
        elif level < last:
            part = call(
                functools.partial(own_kernel, level),
                [mixed],
                coefficients,
                perms,
                blocks,
            )
    half_wide = ((half, width), wide)
    plan_like = [((2 * levels, half, half), thin), ((2 * levels, half, lanes), thin)]
    part, arrived_map, bracket, *plans = call(
        functools.partial(bracket_kernel, last),
        [half_wide, ((width, width), thin), sent] + plan_like,
        coefficients,
        perms,
        own_map,
        blocks,
        early,
        own_slots,
        out_slots,
        arrived_map,
        far=(echoes, source_leaf, pulse_slot),
        scratch=[pltpu.VMEM((half, 2 * width), wide), pltpu.VMEM((half, 2 * width), thin)]
        + echo_scratch,
    )
    arrived_bracket = swapped(bracket, "box", last)
    *plans, rest = call(
        plan_kernel,
        plan_like + [half_wide],
        perms,
        own_slots,
        out_slots,
        *plans,
        outgoing,
        arrived_map,
        aliases={3: 0, 4: 1},
    )
    placed = call(
        functools.partial(join_kernel, last), [column_of], arrived, part, other_map, *plans
    )
    arrived, more = arrived_bracket, (rest,)
    for level in reversed(range(last)):
        coefficients, outgoing = call(
            functools.partial(backward_kernel, level),
            [column_of, sent],
            arrived,
            placed,
            *plans,
            blocks,
            *more,
        )
        arrived, more = swapped(outgoing, "box", level), ()
        placed = call(
            functools.partial(own_back_kernel, level), [column_of], coefficients, blocks, *plans
        )
    return call(
        last_kernel,
        [((rows, samples), thin)],
        arrived,
        placed,
        *plans,
        leaf_near,
        scene_near,
        far_out=True,
        scratch=[
            pltpu.VMEM((rows, samples), thin),
            pltpu.SemaphoreType.DMA((scene_chunks,)),
        ],
    )


def solution(mesh):
    return jax.shard_map(
        on_device,
        mesh=mesh,
        in_specs=(
            P(("groups", "box"), None),
            P(("groups", "box"), None),
            P(("groups", "box"), None),
            P(("groups", "box"), None),
            P(None, "box", None),
            P(),
            P(),
            P(None, "box", None, None, None),
        ),
        out_specs=P(("groups", "box"), None),
        check_vma=False,
    )
```
